256 devices in a mesh: dp: 64 (over y, x_hi, z), emb: 4 (over x_lo, core).
Axes of the slice: x: 4 (x_hi: 2, x_lo: 2; x = x_hi * 2 + x_lo), y: 4, z: 8, core: 2. Of those that a mesh axis runs over, the one named last changes fastest.
Arguments:
- visual_features: bfloat16 [8192, 1280], P('dp'), may hold values from -10 to 10
- sound_features: bfloat16 [8192, 1280], P('dp'), may hold values from -10 to 10
- tactile_features: bfloat16 [8192, 1280], P('dp'), may hold values from -10 to 10
- visual_mapping_matrix: bfloat16 [1280, 1024], P(None, 'emb'), may hold values from -1 to 1
- sound_mapping_matrix: bfloat16 [1280, 1024], P(None, 'emb'), may hold values from -1 to 1
- tactile_mapping_matrix: bfloat16 [1280, 1024], P(None, 'emb'), may hold values from -1 to 1
- couple_sharpness: float32 [3], replicated, may hold values from 10 to 30
Outputs:
- total_loss: float32 [], replicated
- video_grad: float32 [1280, 1024], P('dp', 'emb')
- audio_head_gradient: float32 [1280, 1024], P('dp', 'emb')
- touch_grad: float32 [1280, 1024], P('dp', 'emb')
The draws below stay inside these ranges and needn't reach their ends.
All inputs are finite; a program needn't handle non-finite values.
Results may differ from the reference program's by a relative error of at most 0.0025.
The reference program's roundings to bfloat16 on the way count: a program that leaves them out, or rounds other values in their place, can miss the bound.
Values may be sent and summed in bfloat16 or wider, within the bound.
No kernel may reach another device: no remote copies, remote signals or barrier semaphores. Data moves between devices by JAX's collectives and lax.ppermute only.
A program may use at most 128 MiB of HBM per device.

```python
import math
import jax
import jax.numpy as jnp
from jax import lax

FEAT = 1280
EMBED = 1024
BATCH = 8192


def clip_latent(key):
    keys = jax.random.split(key, 2)
    strength = jax.random.uniform(keys[1], (BATCH, 1), jnp.float32)
    return (keys[0], strength)


def head_common(key):
    return jax.random.fold_in(key, 500)


def gaussian_draw(key, rows, columns):
    return jnp.clip(jax.random.normal(key, (rows, columns), jnp.float32), -4.0, 4.0)


def mix_features(latent, noise, align):
    rest = jnp.sqrt(jnp.maximum(1.0 - align * align, 0.0))
    return (align * latent + rest * noise).astype(jnp.bfloat16)


def mix_head(common, own):
    return ((0.894427 * common + 0.447214 * own) * FEAT ** (-0.5)).astype(jnp.bfloat16)


def draw_visual_features(key, part):
    latent_key, strength = clip_latent(key)
    key = jax.random.fold_in(key, 11)
    return mix_features(gaussian_draw(latent_key, BATCH, FEAT), gaussian_draw(key, BATCH, FEAT), 0.5 + 0.5 * strength)


def draw_sound_features(key, part):
    latent_key, strength = clip_latent(key)
    key = jax.random.fold_in(key, 12)
    return mix_features(gaussian_draw(latent_key, BATCH, FEAT), gaussian_draw(key, BATCH, FEAT), 0.5 + 0.5 * strength)


def draw_tactile_features(key, part):
    latent_key, strength = clip_latent(key)
    key = jax.random.fold_in(key, 13)
    return mix_features(gaussian_draw(latent_key, BATCH, FEAT), gaussian_draw(key, BATCH, FEAT), 0.5 + 0.5 * strength)


def draw_visual_mapping_matrix(key, part):
    common_key = head_common(key)
    key = jax.random.fold_in(key, 21)
    return mix_head(gaussian_draw(common_key, FEAT, EMBED), gaussian_draw(key, FEAT, EMBED))


def draw_sound_mapping_matrix(key, part):
    common_key = head_common(key)
    key = jax.random.fold_in(key, 22)
    return mix_head(gaussian_draw(common_key, FEAT, EMBED), gaussian_draw(key, FEAT, EMBED))


def draw_tactile_mapping_matrix(key, part):
    common_key = head_common(key)
    key = jax.random.fold_in(key, 23)
    return mix_head(gaussian_draw(common_key, FEAT, EMBED), gaussian_draw(key, FEAT, EMBED))


def setup_inputs(seed: int = 0) -> dict:
    key_list = jax.random.split(jax.random.key(seed), 8)
    visual_features = draw_visual_features(jax.random.fold_in(key_list[7], 71), 0)
    sound_features = draw_sound_features(jax.random.fold_in(key_list[7], 71), 0)
    tactile_features = draw_tactile_features(jax.random.fold_in(key_list[7], 71), 0)
    visual_mapping_matrix = draw_visual_mapping_matrix(jax.random.fold_in(key_list[7], 71), 0)
    sound_mapping_matrix = draw_sound_mapping_matrix(jax.random.fold_in(key_list[7], 71), 0)
    tactile_mapping_matrix = draw_tactile_mapping_matrix(jax.random.fold_in(key_list[7], 71), 0)
    couple_sharpness = jnp.clip(jnp.exp(jax.random.uniform(key_list[6], (3,), jnp.float32, math.log(10.0), math.log(30.0))), 10.0, 30.0)
    return {"visual_features": visual_features, "sound_features": sound_features, "tactile_features": tactile_features, "visual_mapping_matrix": visual_mapping_matrix, "sound_mapping_matrix": sound_mapping_matrix, "tactile_mapping_matrix": tactile_mapping_matrix, "couple_sharpness": couple_sharpness}


epsilon = 1e-06
couples = ((0, 1), (0, 2), (1, 2))

def normalize(embedded):
    values = embedded.astype(jnp.float32)
    length = jnp.sqrt(lax.optimization_barrier(jnp.sum(values * values, axis=1, keepdims=True)) + epsilon)
    return (values / length, length)

def reference(visual_features, sound_features, tactile_features, visual_mapping_matrix, sound_mapping_matrix, tactile_mapping_matrix, couple_sharpness):
    inputs = (visual_features, sound_features, tactile_features)
    weights = (visual_mapping_matrix, sound_mapping_matrix, tactile_mapping_matrix)
    embedded = [jnp.dot(sample, matrix, preferred_element_type=jnp.float32).astype(jnp.bfloat16) for sample, matrix in zip(inputs, weights)]
    normed = [normalize(item) for item in embedded]
    unit_rows = [normed_pair[0].astype(jnp.bfloat16) for normed_pair in normed]
    batch_row_count = visual_features.shape[0]
    emb_width = visual_mapping_matrix.shape[1]
    block_rows = min(1024, batch_row_count)
    count_blocks = batch_row_count // block_rows
    column_ids = jnp.arange(batch_row_count, dtype=jnp.int32)
    total_loss = jnp.zeros((), jnp.float32)
    grads = [jnp.zeros((batch_row_count, emb_width), jnp.float32) for modality in range(3)]
    for sense_couple, (source, target) in enumerate(couples):
        logit_multiplier = couple_sharpness[sense_couple]
        left_units = unit_rows[source]
        right_units = unit_rows[target]

        def scores_of(start, left_units=left_units, right_units=right_units, logit_multiplier=logit_multiplier):
            row_part = lax.dynamic_slice_in_dim(left_units, start, block_rows, 0)
            scores = logit_multiplier * lax.dot_general(row_part, right_units, (((1,), (1,)), ((), ())), preferred_element_type=jnp.float32)
            return (scores, row_part)

        def forward(column_sum, step_index, scores_of=scores_of, logit_multiplier=logit_multiplier):
            scores, row_part = scores_of(step_index * block_rows)
            shifted = jnp.exp(scores - logit_multiplier)
            return (column_sum + lax.optimization_barrier(jnp.sum(shifted, axis=0)), logit_multiplier + jnp.log(lax.optimization_barrier(jnp.sum(shifted, axis=1))))
        column_sum, row_lse = lax.scan(forward, jnp.zeros((batch_row_count,), jnp.float32), jnp.arange(count_blocks, dtype=jnp.int32))
        row_lse = row_lse.reshape(batch_row_count)
        column_lse = logit_multiplier + jnp.log(column_sum)
        diagonal = logit_multiplier * lax.optimization_barrier(jnp.sum(left_units.astype(jnp.float32) * right_units.astype(jnp.float32), axis=1))
        total_loss = total_loss + (jnp.sum(row_lse - diagonal) + jnp.sum(column_lse - diagonal)) / (2 * batch_row_count)

        def backward(target_grad, step_index, scores_of=scores_of, row_lse=row_lse, column_lse=column_lse, right_units=right_units, logit_multiplier=logit_multiplier):
            start = step_index * block_rows
            scores, row_part = scores_of(start)
            row_stats = lax.dynamic_slice_in_dim(row_lse, start, block_rows, 0)
            row_ids = start + jnp.arange(block_rows, dtype=jnp.int32)
            positive = (row_ids[:, None] == column_ids[None, :]).astype(jnp.float32)
            gradient = (0.5 * (jnp.exp(scores - row_stats[:, None]) + jnp.exp(scores - column_lse[None, :])) - positive).astype(jnp.bfloat16)
            source_part = logit_multiplier * jnp.dot(gradient, right_units, preferred_element_type=jnp.float32)
            target_grad = target_grad + logit_multiplier * lax.dot_general(gradient, row_part, (((0,), (0,)), ((), ())), preferred_element_type=jnp.float32)
            return (target_grad, source_part)
        target_grad, source_parts = lax.scan(backward, jnp.zeros((batch_row_count, emb_width), jnp.float32), jnp.arange(count_blocks, dtype=jnp.int32))
        grads[source] = grads[source] + source_parts.reshape(batch_row_count, emb_width)
        grads[target] = grads[target] + target_grad
    results = []
    for modality in range(3):
        unit_value, length = normed[modality]
        inner_dot = lax.optimization_barrier(jnp.sum(unit_value * grads[modality], axis=1, keepdims=True))
        demb = ((grads[modality] - unit_value * inner_dot) / length).astype(jnp.bfloat16)
        results.append(lax.dot_general(inputs[modality], demb, (((0,), (0,)), ((), ())), preferred_element_type=jnp.float32))
    return (total_loss, results[0], results[1], results[2])
```

```python
import jax
import jax.numpy as jnp
from jax import lax
from jax.sharding import Mesh, PartitionSpec as P

epsilon = 1e-06
couples = ((0, 1), (0, 2), (1, 2))
EMB = ("xl", "core")
DP = ("y", "xh", "z")
ROW = ("y", "xh", "xl")
COL = ("z", "core")
NEAR = ("y", "xl", "core")
bf16 = jnp.bfloat16
f32 = jnp.float32


def exchange(pieces, axes):
    return lax.all_to_all(pieces, axes, split_axis=0, concat_axis=0, tiled=True)


def spread(value, axes):
    count = lax.axis_size(axes)
    return exchange(jnp.broadcast_to(value[None], (count, *value.shape)), axes)


def contract(left, right, dims):
    return lax.dot_general(left, right, (dims, ((), ())), preferred_element_type=f32)


def shards(f0, f1, f2, h0, h1, h2, sharpness):
    features, heads = (f0, f1, f2), (h0, h1, h2)
    clips, feat = f0.shape
    quarter = h0.shape[1]
    emb_size = lax.axis_size(EMB)
    near_y = lax.axis_size("y")
    n_row, n_col = lax.axis_size(ROW), lax.axis_size(COL)
    own = clips // emb_size
    width = quarter * emb_size
    block_r, block_c = n_row * own, n_col * own

    slices = jnp.stack([f.reshape(clips, near_y, feat // near_y) for f in features], axis=0)
    slices = slices.transpose(2, 0, 3, 1)
    my_y = lax.axis_index("y")
    wide = [lax.dynamic_index_in_dim(slices, my_y, 0, keepdims=False)]
    for step in range(1, near_y):
        piece = lax.dynamic_index_in_dim(slices, (my_y + step) % near_y, 0, keepdims=False)
        wide.append(
            lax.ppermute(piece, "y", [(i, (i + step) % near_y) for i in range(near_y)])
        )

    emb = jnp.stack(
        [contract(f, h, ((1,), (0,))).astype(bf16) for f, h in zip(features, heads)]
    )
    emb = emb.reshape(3, emb_size, own, quarter).transpose(1, 0, 2, 3)
    emb = exchange(emb, EMB).transpose(1, 2, 0, 3).reshape(3, own, width)
    values = emb.astype(f32)
    length = jnp.sqrt(jnp.sum(values * values, axis=2, keepdims=True) + epsilon)
    unit_value = values / length
    u = lax.reduce_precision(unit_value, 8, 7)
    unit = u.astype(bf16)

    cols = lax.all_gather(unit[1:], COL, axis=0)
    rows = spread(unit[:2], ROW)
    rows, wide = lax.optimization_barrier((rows, wide))
    r0, r1 = rows[:, 0].reshape(block_r, width), rows[:, 1].reshape(block_r, width)
    c1, c2 = cols[:, 0].reshape(block_c, width), cols[:, 1].reshape(block_c, width)

    t = [sharpness[p] for p in range(3)]
    pairs = ((r0, c1), (r0, c2), (r1, c2))
    shifted = [
        jnp.exp(t[p] * contract(a, b, ((1,), (1,))) - t[p]) for p, (a, b) in enumerate(pairs)
    ]
    self_score = [
        t[p] * jnp.sum(u[a] * u[b], axis=1, keepdims=True) for p, (a, b) in enumerate(couples)
    ]
    diagonal = sum(jnp.sum(d) for d in self_score)
    row_part = jnp.stack(
        [jnp.sum(e, axis=1) for e in shifted] + [jnp.full((block_r,), diagonal)]
    )
    col_part = jnp.stack([jnp.sum(e, axis=0) for e in shifted])
    row_sum = jnp.sum(spread(row_part, ROW), axis=0)
    col_sum = jnp.sum(spread(col_part, COL), axis=0)

    scale = 1.0 / (2 * clips * lax.axis_size(DP))
    row_lse = sum(block_r * t[p] + jnp.sum(jnp.log(row_sum[p])) for p in range(3))
    col_lse = sum(block_c * t[p] + jnp.sum(jnp.log(col_sum[p])) for p in range(3))
    loss = ((row_lse - 2.0 * row_sum[3, 0]) / n_row + col_lse / n_col) * scale

    my_row, my_col = lax.axis_index(ROW), lax.axis_index(COL)
    row_id = lax.broadcasted_iota(jnp.int32, (block_r, block_c), 0) - my_row * own
    col_id = lax.broadcasted_iota(jnp.int32, (block_r, block_c), 1) - my_col * own
    other = jnp.where((row_id == col_id) & (row_id >= 0) & (row_id < own), 0.0, 1.0)
    grad = [
        (
            other * shifted[p] * (0.5 / row_sum[p][:, None] + 0.5 / col_sum[p][None, :])
        ).astype(bf16)
        for p in range(3)
    ]
    self_grad = []
    for p in range(3):
        z_row = lax.dynamic_slice_in_dim(row_sum[p], my_row * own, own, 0)[:, None]
        z_col = lax.dynamic_slice_in_dim(col_sum[p], my_col * own, own, 0)[:, None]
        e_self = jnp.exp(self_score[p] - t[p])
        g_self = e_self * (0.5 / z_row + 0.5 / z_col) - 1.0
        self_grad.append(t[p] * lax.reduce_precision(g_self, 8, 7))
    d_r0 = t[0] * contract(grad[0], c1, ((1,), (0,))) + t[1] * contract(grad[1], c2, ((1,), (0,)))
    d_r1 = t[2] * contract(grad[2], c2, ((1,), (0,)))
    d_c1 = t[0] * contract(grad[0], r0, ((0,), (0,)))
    d_c2 = t[1] * contract(grad[1], r0, ((0,), (0,))) + t[2] * contract(grad[2], r1, ((0,), (0,)))

    d_cols = jnp.stack([d_c1.reshape(n_col, own, width), d_c2.reshape(n_col, own, width)], axis=1)
    d_rows = jnp.stack([d_r0.reshape(n_row, own, width), d_r1.reshape(n_row, own, width)], axis=1)
    n_z = lax.axis_size("z")
    my_core = lax.axis_index("core")
    d_cols = d_cols.reshape(n_z, 2, 2 * own, width)
    mine = lax.dynamic_index_in_dim(d_cols, my_core, 1, keepdims=False)
    theirs = lax.dynamic_index_in_dim(d_cols, 1 - my_core, 1, keepdims=False)
    mine = mine + lax.ppermute(theirs, "core", [(0, 1), (1, 0)])
    d_cols = lax.psum_scatter(mine, "z", scatter_dimension=0).reshape(2, own, width)
    d_rows = jnp.sum(exchange(d_rows.astype(bf16), ROW).astype(f32), axis=0)
    d_unit = jnp.stack(
        [
            d_rows[0] + self_grad[0] * u[1] + self_grad[1] * u[2],
            d_rows[1] + d_cols[0] + self_grad[0] * u[0] + self_grad[2] * u[2],
            d_cols[1] + self_grad[1] * u[0] + self_grad[2] * u[1],
        ]
    )

    inner = jnp.sum(unit_value * d_unit, axis=2, keepdims=True)
    d_emb = ((d_unit - unit_value * inner) / length).astype(bf16)

    parts = []
    rest = loss
    for _ in range(3):
        part = lax.reduce_precision(rest, 8, 7)
        parts.append(part.astype(bf16))
        rest = rest - part
    tail = jnp.stack(parts + [jnp.zeros((), bf16)] * 13)
    tail = jnp.broadcast_to(tail[:, None], (16, quarter))
    d_emb = d_emb.reshape(3 * own, emb_size, quarter).transpose(1, 0, 2)
    d_emb = jnp.concatenate(
        [d_emb, jnp.broadcast_to(tail[None], (emb_size, 16, quarter))], axis=1
    )
    height = d_emb.shape[1]
    d_emb = jnp.broadcast_to(d_emb[None], (near_y, *d_emb.shape))
    d_emb = exchange(d_emb.reshape(near_y * emb_size, height, quarter), NEAR)
    loss = jnp.sum(d_emb[:, 3 * own : 3 * own + 3, 0].astype(f32))
    d_emb = d_emb.reshape(near_y, emb_size, height, quarter)
    partial = []
    for m in range(3):
        total = jnp.zeros((feat // near_y, quarter), f32)
        for step in range(near_y):
            source = (my_y - step) % near_y
            there = lax.dynamic_index_in_dim(d_emb, source, 0, keepdims=False)
            there = there[:, m * own : (m + 1) * own].reshape(clips, quarter)
            total = total + contract(wide[step][m], there, ((1,), (0,)))
        partial.append(total)

    n_x = lax.axis_size("xh")
    share = feat // near_y // n_x // n_z
    partial = jnp.stack([p.reshape(n_x, n_z, share, quarter) for p in partial], axis=2)
    partial = partial.reshape(n_x, n_z, 3 * share, quarter)
    extra = jnp.broadcast_to(loss, (n_x, n_z, 4, quarter))
    partial = jnp.concatenate([partial, extra], axis=2)
    my_x = lax.axis_index("xh")
    kept = lax.dynamic_index_in_dim(partial, my_x, 0, keepdims=False)
    sent = lax.dynamic_index_in_dim(partial, 1 - my_x, 0, keepdims=False)
    kept = kept + lax.ppermute(sent, "xh", [(0, 1), (1, 0)])
    kept = jnp.sum(exchange(kept, "z"), axis=0)
    out = kept[: 3 * share].reshape(3, share, quarter)
    return kept[3 * share, 0], out[0], out[1], out[2]


def solution(mesh):
    fine = Mesh(mesh.devices.reshape(4, 2, 8, 2, 2), ("y", "xh", "z", "xl", "core"))
    clip_rows, columns = P(DP, None), P(None, EMB)
    out = P(DP, EMB)
    return jax.shard_map(
        shards,
        mesh=fine,
        in_specs=(clip_rows,) * 3 + (columns,) * 3 + (P(),),
        out_specs=(P(), out, out, out),
        check_vma=False,
    )
```

```python
import functools

import jax
import jax.numpy as jnp
import numpy as np
from jax import lax
from jax.experimental import pallas as pl
from jax.experimental.pallas import tpu as pltpu
from jax.sharding import Mesh, PartitionSpec as P

epsilon = 1e-06
couples = ((0, 1), (0, 2), (1, 2))
EMB = ("xl", "core")
DP = ("y", "xh", "z")
ROW = ("y", "xh", "xl")
COL = ("z", "core")
NEAR = ("y", "xl", "core")
FAR = ("xh", "z")
bf16 = jnp.bfloat16
f32 = jnp.float32
LANES = 128
TILE = 128
SCORE_TILE = 256


def exchange(pieces, axes):
    return lax.all_to_all(pieces, axes, split_axis=0, concat_axis=0, tiled=True)


def spread(value, axes):
    count = lax.axis_size(axes)
    return exchange(jnp.broadcast_to(value[None], (count, *value.shape)), axes)


def contract(left, right, dims):
    return lax.dot_general(left, right, (dims, ((), ())), preferred_element_type=f32)


def call(kernel, grid, in_specs, out_specs, out_shape, scratch=(), flops=0, room=32):
    return pl.pallas_call(
        kernel,
        grid=grid,
        in_specs=in_specs,
        out_specs=out_specs,
        out_shape=out_shape,
        scratch_shapes=scratch,
        compiler_params=pltpu.CompilerParams(vmem_limit_bytes=room * 2**20),
        cost_estimate=pl.CostEstimate(flops=flops, bytes_accessed=8 * 2**20, transcendentals=0),
    )


def whole(shape):
    return pl.BlockSpec(shape, lambda *_: (0,) * len(shape))


scalars = pl.BlockSpec(memory_space=pltpu.SMEM)


def share_kernel(share, line, at_ref, f0_ref, f1_ref, f2_ref, own_ref, *send_refs):
    n_y = 1 + len(send_refs)
    rows, feat = own_ref.shape[2], f0_ref.shape[1]
    r = lax.broadcasted_iota(jnp.int32, (rows, 1), 0)
    place = r // line
    inside = r - place * line < share
    column = lax.broadcasted_iota(jnp.int32, (rows, feat), 1)
    jobs = [(own_ref.at[x], 0, x) for x in range(2)]
    jobs += [(ref, step, at_ref[2]) for step, ref in enumerate(send_refs, 1)]
    for ref, step, x in jobs:
        start = (2 * lax.rem(at_ref[3] + step, n_y) + x) * (feat // n_y // 2)
        target = jnp.where(inside, r - place * (line - share) + start, -1)
        pick = jnp.where(column == target, 1.0, 0.0).astype(bf16)
        for m, f_ref in enumerate((f0_ref, f1_ref, f2_ref)):
            ref[m] = contract(pick, f_ref[...], ((1,), (1,))).astype(bf16)


def feature_shares(at, features, n_y, n_z, line):
    clips, feat = features[0].shape
    share = feat // n_y // n_z // 2
    shape = (3, n_z * line, clips)
    shapes = [(2, *shape)] + [shape] * (n_y - 1)
    return call(
        functools.partial(share_kernel, share, line),
        (1,),
        [scalars] + [whole(f.shape) for f in features],
        [whole(x) for x in shapes],
        [jax.ShapeDtypeStruct(x, bf16) for x in shapes],
        flops=6 * n_y * n_z * line * feat * clips,
    )(at, *features)


def unit_kernel(t_ref, emb_ref, all_ref, unit_ref, rows_ref, cols_ref, own_ref):
    parts, _, own, quarter = emb_ref.shape
    for m in range(3):
        emb = jnp.concatenate([emb_ref[e, m] for e in range(parts)], axis=1)
        values = emb.astype(f32)
        length = jnp.sqrt(jnp.sum(values * values, axis=1, keepdims=True) + epsilon)
        unit = (values / length).astype(bf16)
        all_ref[m] = emb
        unit_ref[m] = unit
        if m > 0:
            cols_ref[m - 1] = unit
        if m < 2:
            for copy in range(rows_ref.shape[0]):
                rows_ref[copy, m] = unit
    total = jnp.zeros((1, parts * quarter), f32)
    for p, (a, b) in enumerate(couples):
        product = unit_ref[a].astype(f32) * unit_ref[b].astype(f32)
        total += t_ref[p] * jnp.sum(product, axis=0, keepdims=True)
    own_ref[...] = jnp.broadcast_to(jnp.sum(total, axis=1, keepdims=True), own_ref.shape)


def units(t, emb, copies):
    parts, _, own, quarter = emb.shape
    full = (3, own, parts * quarter)
    shapes = [full, full, (copies, 2, *full[1:]), (2, *full[1:])]
    return call(
        unit_kernel,
        (1,),
        [scalars, whole(emb.shape)],
        [whole(x) for x in shapes] + [whole((8, LANES))],
        [jax.ShapeDtypeStruct(x, bf16) for x in shapes] + [jax.ShapeDtypeStruct((8, LANES), f32)],
        flops=10**6,
    )(t, emb)


def score_kernel(t_ref, rows_ref, cols_ref, own_ref, e_ref, row_ref, col_ref):
    step = pl.program_id(0)
    own, width = rows_ref.shape[2], rows_ref.shape[3]
    rows = [rows_ref[:, m].reshape(SCORE_TILE, width) for m in range(2)]
    cols = [cols_ref[:, m].reshape(cols_ref.shape[0] * own, width) for m in range(2)]

    @pl.when(step == 0)
    def _():
        col_ref[...] = jnp.zeros_like(col_ref)

    row_ref[...] = jnp.broadcast_to(own_ref[:, 0:1], row_ref.shape)
    for p, (a, b) in enumerate(((0, 0), (0, 1), (1, 1))):
        t = t_ref[p]
        e = jnp.exp(t * contract(rows[a], cols[b], ((1,), (1,))) - t)
        e_ref[p] = e
        col_ref[p : p + 1, :] += jnp.sum(e, axis=0, keepdims=True)
        total = jnp.broadcast_to(jnp.sum(e, axis=1, keepdims=True), (SCORE_TILE, LANES))
        row_ref[p : p + 1, :] = total.T[0:1]


def scores(t, rows, cols, own_scores):
    n_row, _, own, width = rows.shape
    n_col = cols.shape[0]
    block_r, block_c = n_row * own, n_col * own
    per = SCORE_TILE // own
    return call(
        score_kernel,
        (block_r // SCORE_TILE,),
        [
            scalars,
            pl.BlockSpec((per, 2, own, width), lambda i: (i, 0, 0, 0)),
            whole(cols.shape),
            whole(own_scores.shape),
        ],
        [
            pl.BlockSpec((3, SCORE_TILE, block_c), lambda i: (0, i, 0)),
            pl.BlockSpec((8, SCORE_TILE), lambda i: (0, i)),
            whole((8, block_c)),
        ],
        [
            jax.ShapeDtypeStruct((3, block_r, block_c), f32),
            jax.ShapeDtypeStruct((8, block_r), f32),
            jax.ShapeDtypeStruct((8, block_c), f32),
        ],
        flops=6 * block_r * block_c * width,
        room=60,
    )(t, rows, cols, own_scores)


def column_kernel(
    t_ref, at_ref, e_ref, rows_ref, zr_ref, zc_ref, zc_all_ref, g_ref, keep_ref, send_ref, w_ref, hr_ref
):
    step = pl.program_id(0)
    n_row, own, width = rows_ref.shape[0], rows_ref.shape[2], rows_ref.shape[3]
    block_r = n_row * own
    my_row, my_col, my_core = at_ref[0], at_ref[1], at_ref[2]

    @pl.when(step == 0)
    def _():
        for p in range(3):
            half = jnp.broadcast_to(0.5 / zr_ref[p : p + 1, :], (LANES, block_r))
            hr_ref[p] = half.T
            half = jnp.broadcast_to(0.5 / zc_all_ref[p : p + 1, :], (LANES, zc_all_ref.shape[1]))
            hr_ref[3] = half.T
            w_ref[p] = (
                hr_ref[p, pl.ds(pl.multiple_of(my_row * own, own), own), :]
                + hr_ref[3, pl.ds(pl.multiple_of(my_col * own, own), own), :]
            )

    row_id = lax.broadcasted_iota(jnp.int32, (block_r, TILE), 0) - my_row * own
    col_id = lax.broadcasted_iota(jnp.int32, (block_r, TILE), 1) + (step * TILE - my_col * own)
    own_term = (row_id == col_id) & (row_id >= 0) & (row_id < own)
    rows = [rows_ref[:, m].reshape(block_r, width) for m in range(2)]
    grads = []
    for p in range(3):
        g = e_ref[p] * (hr_ref[p] + 0.5 / zc_ref[p : p + 1, :])
        g = jnp.where(own_term, 0.0, g).astype(bf16)
        g_ref[p] = g
        grads.append(g)
    d1 = t_ref[0] * contract(grads[0], rows[0], ((0,), (0,)))
    d2 = t_ref[1] * contract(grads[1], rows[0], ((0,), (0,)))
    d2 += t_ref[2] * contract(grads[2], rows[1], ((0,), (0,)))
    for i in range(TILE // (2 * own)):
        for m, d in enumerate((d1, d2)):
            low = d[2 * i * own : (2 * i + 1) * own]
            high = d[(2 * i + 1) * own : (2 * i + 2) * own]
            keep_ref[i, m] = jnp.where(my_core == 0, low, high)
            send_ref[i, m] = jnp.where(my_core == 0, high, low).astype(bf16)


def column_gradients(t, at, e, rows, zr, zc):
    n_row, _, own, width = rows.shape
    _, block_r, block_c = e.shape
    half = block_c // own // 2
    per = TILE // (2 * own)
    tiles = lambda i: (i, 0, 0, 0)
    return call(
        column_kernel,
        (block_c // TILE,),
        [
            scalars,
            scalars,
            pl.BlockSpec((3, block_r, TILE), lambda i: (0, 0, i)),
            whole(rows.shape),
            whole(zr.shape),
            pl.BlockSpec((4, TILE), lambda i: (0, i)),
            whole(zc.shape),
        ],
        [
            pl.BlockSpec((3, block_r, TILE), lambda i: (0, 0, i)),
            pl.BlockSpec((per, 2, own, width), tiles),
            pl.BlockSpec((per, 2, own, width), tiles),
            whole((3, own, LANES)),
        ],
        [
            jax.ShapeDtypeStruct((3, block_r, block_c), bf16),
            jax.ShapeDtypeStruct((half, 2, own, width), f32),
            jax.ShapeDtypeStruct((half, 2, own, width), bf16),
            jax.ShapeDtypeStruct((3, own, LANES), f32),
        ],
        [pltpu.VMEM((4, max(block_r, block_c), LANES), f32)],
        flops=6 * block_r * block_c * width,
        room=60,
    )(t, at, e, rows, zr, zc, zc)


def row_kernel(t_ref, g_ref, cols_ref, out_ref):
    per, own, width = out_ref.shape[0], out_ref.shape[2], out_ref.shape[3]
    cols = [cols_ref[:, m].reshape(cols_ref.shape[0] * own, width) for m in range(2)]
    d0 = t_ref[0] * contract(g_ref[0], cols[0], ((1,), (0,)))
    d0 += t_ref[1] * contract(g_ref[1], cols[1], ((1,), (0,)))
    d1 = t_ref[2] * contract(g_ref[2], cols[1], ((1,), (0,)))
    out_ref[:, 0] = d0.astype(bf16).reshape(per, own, width)
    out_ref[:, 1] = d1.astype(bf16).reshape(per, own, width)


def row_gradients(t, g, cols):
    n_col, _, own, width = cols.shape
    _, block_r, block_c = g.shape
    per = TILE // own
    return call(
        row_kernel,
        (block_r // TILE,),
        [scalars, pl.BlockSpec((3, TILE, block_c), lambda i: (0, i, 0)), whole(cols.shape)],
        pl.BlockSpec((per, 2, own, width), lambda i: (i, 0, 0, 0)),
        jax.ShapeDtypeStruct((block_r // own, 2, own, width), bf16),
        flops=6 * block_r * block_c * width,
        room=60,
    )(t, g, cols)


def exact_parts(value, rows):
    line = lax.broadcasted_iota(jnp.int32, (rows, value.shape[1]), 0)
    rest = jnp.broadcast_to(value, line.shape)
    out = jnp.zeros(line.shape, f32)
    for i in range(3):
        part = rest.astype(bf16).astype(f32)
        out = jnp.where(line == i, part, out)
        rest = rest - part
    return out


def embed_kernel(
    n_row, n_col, scale, t_ref, rows_ref, cols_ref, emb_ref, unit_ref, w_ref, zr_ref, zc_ref, out_ref
):
    copies, parts = out_ref.shape[0], out_ref.shape[1]
    own, width = emb_ref.shape[1], emb_ref.shape[2]
    quarter = width // parts
    sums = [jnp.zeros((own, width), f32) for _ in range(2)]
    for i in range(rows_ref.shape[0]):
        for m in range(2):
            sums[m] += rows_ref[i, m].astype(f32)
    d_unit = [sums[0], sums[1] + cols_ref[0], cols_ref[1]]
    unit = [unit_ref[m].astype(f32) for m in range(3)]
    for p, (a, b) in enumerate(couples):
        t = t_ref[p]
        score = t * jnp.sum(unit[a] * unit[b], axis=1, keepdims=True)
        g = (jnp.exp(score - t) * w_ref[p][:, 0:1] - 1.0).astype(bf16).astype(f32)
        d_unit[a] += (t * g) * unit[b]
        d_unit[b] += (t * g) * unit[a]
    for m in range(3):
        values = emb_ref[m].astype(f32)
        length = jnp.sqrt(jnp.sum(values * values, axis=1, keepdims=True) + epsilon)
        value = values / length
        inner = jnp.sum(value * d_unit[m], axis=1, keepdims=True)
        d = ((d_unit[m] - value * inner) / length).astype(bf16)
        for c in range(copies):
            for e in range(parts):
                out_ref[c, e, m * own : (m + 1) * own, :] = d[:, e * quarter : (e + 1) * quarter]
    loss = -2.0 / n_row * zr_ref[3:4, 0:1]
    for p in range(3):
        for z_ref, count in ((zr_ref, n_row), (zc_ref, n_col)):
            lse = t_ref[p] + jnp.log(z_ref[p : p + 1, :])
            loss += jnp.sum(lse, axis=1, keepdims=True) * (1.0 / count)
    tail = exact_parts(jnp.broadcast_to(loss * scale, (1, quarter)), 16).astype(bf16)
    for c in range(copies):
        for e in range(parts):
            out_ref[c, e, 3 * own : 3 * own + 16, :] = tail


def embed_gradients(t, rows, cols, emb, unit, w, zr, zc, copies, parts, total):
    _, own, width = emb.shape
    shape = (copies, parts, 3 * own + 16, width // parts)
    kernel = functools.partial(
        embed_kernel, zr.shape[1] // own, zc.shape[1] // own, 1.0 / (2 * total)
    )
    return call(
        kernel,
        (1,),
        [scalars] + [whole(x.shape) for x in (rows, cols, emb, unit, w, zr, zc)],
        whole(shape),
        jax.ShapeDtypeStruct(shape, bf16),
        flops=10**6,
    )(t, rows, cols, emb, unit, w, zr, zc)


def head_kernel(share, line, at_ref, d_ref, own_ref, mine_ref, other_ref, out_ref):
    n_y = 1 + mine_ref.shape[0]
    my_core, my_y = at_ref[2], at_ref[3]
    n_far, height, quarter = out_ref.shape
    n_z = n_far // 2
    parts = d_ref.shape[0] // n_y
    own = (d_ref.shape[1] - 16) // 3
    clips = parts * own
    tail = jnp.sum(d_ref[:, 3 * own : 3 * own + 16, :].astype(f32), axis=0)
    loss = exact_parts(jnp.sum(tail, axis=0, keepdims=True), 8)[: height - 3 * share]
    totals = []
    for m in range(3):
        there = [
            d_ref[
                pl.ds(lax.rem(my_y + (n_y - step), n_y) * parts, parts), m * own : (m + 1) * own, :
            ].reshape(clips, quarter)
            for step in range(n_y)
        ]
        there = jnp.concatenate(there, axis=0)
        mine = [mine_ref[step, m] for step in range(n_y - 1)]
        other = [other_ref[step, m] for step in range(n_y - 1)]
        for x in range(2):
            here = [jnp.where(my_core == x, a, b) for a, b in zip(mine, other)]
            here = jnp.concatenate([own_ref[x, m]] + here, axis=1)
            totals.append(contract(here, there, ((1,), (0,))))
    for far in range(n_far):
        x, z = far // n_z, far % n_z
        piece = [totals[2 * m + x][z * line : z * line + share] for m in range(3)]
        out_ref[far] = jnp.concatenate(piece + [loss], axis=0).astype(bf16)


def head_gradients(at, d, own, mine, other, share, line):
    n_z = own.shape[2] // line
    quarter = d.shape[2]
    shape = (2 * n_z, -(-(3 * share + 3) // 16) * 16, quarter)
    return call(
        functools.partial(head_kernel, share, line),
        (1,),
        [scalars] + [whole(x.shape) for x in (d, own, mine, other)],
        whole(shape),
        jax.ShapeDtypeStruct(shape, bf16),
        flops=10**9,
    )(at, d, own, mine, other)


def summing_groups(n_y, n_x, n_z, n_l):
    ids = np.arange(n_y * n_x * n_z * n_l * 2).reshape(n_y, n_x, n_z, n_l, 2)
    over_z = ids[..., 0].reshape(n_y * n_x, n_z * n_l)
    over_plane = ids[..., 1].transpose(2, 0, 1, 3).reshape(n_z, n_y * n_x * n_l)
    return over_z.tolist() + over_plane.tolist()


def shards(f0, f1, f2, h0, h1, h2, sharpness):
    features, heads = (f0, f1, f2), (h0, h1, h2)
    clips, feat = f0.shape
    quarter = h0.shape[1]
    emb_size = lax.axis_size(EMB)
    n_y, n_x, n_z = lax.axis_size("y"), lax.axis_size("xh"), lax.axis_size("z")
    n_row, n_col = lax.axis_size(ROW), lax.axis_size(COL)
    own = clips // emb_size
    width = quarter * emb_size
    block_r, block_c = n_row * own, n_col * own
    my_y = lax.axis_index("y")
    at = jnp.stack(
        [lax.axis_index(ROW), lax.axis_index(COL), lax.axis_index("core"), my_y, lax.axis_index("xh")]
    ).astype(jnp.int32)

    share = feat // n_y // n_x // n_z
    line = -(-share // 8) * 8
    swap = [(0, 1), (1, 0)]
    wide, *sent = feature_shares(at, features, n_y, n_z, line)
    sent = [
        lax.ppermute(piece, "y", [(i, (i + step) % n_y) for i in range(n_y)])
        for step, piece in enumerate(sent, 1)
    ]
    mine = jnp.stack(sent)
    other = lax.ppermute(mine, "core", swap)

    emb = jnp.stack(
        [contract(f, h, ((1,), (0,))).astype(bf16) for f, h in zip(features, heads)]
    )
    emb = emb.reshape(3, emb_size, own, quarter).transpose(1, 0, 2, 3)
    emb, unit, rows, cols, own_scores = units(sharpness, exchange(emb, EMB), n_row)

    cols = lax.all_gather(cols, COL, axis=0)
    rows = exchange(rows, ROW)
    rows, wide, mine, other = lax.optimization_barrier((rows, wide, mine, other))

    e, row_part, col_part = scores(sharpness, rows, cols, own_scores)
    first = lax.axis_index("core") == 0
    got = lax.ppermute(jnp.where(first, row_part, col_part), "core", swap)
    both = jnp.where(
        first,
        jnp.concatenate([(col_part + got)[:4], jnp.zeros((4, block_c), f32)], axis=0),
        jnp.concatenate([got[:4], row_part[:4]], axis=0),
    )
    groups = summing_groups(n_y, n_x, n_z, 2)
    same = jnp.arange(n_row) % 2 == lax.axis_index("xl")
    weight = jnp.where(first, same.astype(f32), 1.0)
    both = jnp.broadcast_to(both[None], (n_row, *both.shape))
    both, weight = lax.optimization_barrier((both, weight))
    both = lax.all_to_all(
        both, ("y", "xh", "z", "xl", "core"), 0, 0, axis_index_groups=groups, tiled=True
    )
    both = jnp.sum(both * weight[:, None, None], axis=0)
    got = lax.ppermute(both[:4], "core", swap)
    row_sum = jnp.where(first, got, both[4:])
    col_sum = jnp.where(first, both[:4], got)

    grad, keep, send, w = column_gradients(sharpness, at, e, rows, row_sum, col_sum)
    received = lax.ppermute(send, "core", swap)
    d_rows = row_gradients(sharpness, grad, cols)
    received, d_rows = lax.optimization_barrier((received, d_rows))
    d_cols = lax.psum_scatter(keep + received.astype(f32), "z", scatter_dimension=0)
    d_rows = exchange(d_rows, ROW)

    d_emb = embed_gradients(
        sharpness, d_rows, d_cols, emb, unit, w, row_sum, col_sum, n_y, emb_size, clips * lax.axis_size(DP)
    )
    d_emb = exchange(d_emb.reshape(n_y * emb_size, 3 * own + 16, quarter), NEAR)

    out = head_gradients(at, d_emb, wide, mine, other, share, line)
    out = jnp.sum(exchange(out, FAR).astype(f32), axis=0)
    loss = out[3 * share, 0] + out[3 * share + 1, 0] + out[3 * share + 2, 0]
    return loss, out[:share], out[share : 2 * share], out[2 * share : 3 * share]


def solution(mesh):
    fine = Mesh(mesh.devices.reshape(4, 2, 8, 2, 2), ("y", "xh", "z", "xl", "core"))
    clip_rows, columns = P(DP, None), P(None, EMB)
    out = P(DP, EMB)
    return jax.shard_map(
        shards,
        mesh=fine,
        in_specs=(clip_rows,) * 3 + (columns,) * 3 + (P(),),
        out_specs=(P(), out, out, out),
        check_vma=False,
    )
```

```python
import functools

import jax
import jax.numpy as jnp
import numpy as np
from jax import lax
from jax.experimental import pallas as pl
from jax.experimental.pallas import tpu as pltpu
from jax.sharding import Mesh, PartitionSpec as P

epsilon = 1e-06
couples = ((0, 1), (0, 2), (1, 2))
EMB = ("xl", "core")
DP = ("y", "xh", "z")
ROW = ("y", "xh", "xl")
COL = ("z", "core")
NEAR = ("y", "xl", "core")
FAR = ("xh", "z")
bf16 = jnp.bfloat16
f32 = jnp.float32
LANES = 128
TILE = 256


def exchange(pieces, axes):
    return lax.all_to_all(pieces, axes, split_axis=0, concat_axis=0, tiled=True)


def spread(value, axes):
    count = lax.axis_size(axes)
    return exchange(jnp.broadcast_to(value[None], (count, *value.shape)), axes)


def contract(left, right, dims):
    return lax.dot_general(left, right, (dims, ((), ())), preferred_element_type=f32)


def call(kernel, grid, in_specs, out_specs, out_shape, scratch=(), flops=0, room=32):
    return pl.pallas_call(
        kernel,
        grid=grid,
        in_specs=in_specs,
        out_specs=out_specs,
        out_shape=out_shape,
        scratch_shapes=scratch,
        compiler_params=pltpu.CompilerParams(vmem_limit_bytes=room * 2**20),
        cost_estimate=pl.CostEstimate(flops=flops, bytes_accessed=8 * 2**20, transcendentals=0),
    )


def whole(shape):
    return pl.BlockSpec(shape, lambda *_: (0,) * len(shape))


scalars = pl.BlockSpec(memory_space=pltpu.SMEM)


def share_kernel(share, line, at_ref, f0_ref, f1_ref, f2_ref, own_ref, *send_refs):
    n_y = 1 + len(send_refs)
    rows, feat = own_ref.shape[2], f0_ref.shape[1]
    r = lax.broadcasted_iota(jnp.int32, (rows, 1), 0)
    place = r // line
    inside = r - place * line < share
    column = lax.broadcasted_iota(jnp.int32, (rows, feat), 1)
    jobs = [(own_ref.at[x], 0, x) for x in range(2)]
    jobs += [(ref, step, at_ref[2]) for step, ref in enumerate(send_refs, 1)]
    for ref, step, x in jobs:
        start = (2 * lax.rem(at_ref[3] + step, n_y) + x) * (feat // n_y // 2)
        target = jnp.where(inside, r - place * (line - share) + start, -1)
        pick = jnp.where(column == target, 1.0, 0.0).astype(bf16)
        for m, f_ref in enumerate((f0_ref, f1_ref, f2_ref)):
            ref[m] = contract(pick, f_ref[...], ((1,), (1,))).astype(bf16)


def feature_shares(at, features, n_y, n_z, line):
    clips, feat = features[0].shape
    share = feat // n_y // n_z // 2
    shape = (3, n_z * line, clips)
    shapes = [(2, *shape)] + [shape] * (n_y - 1)
    return call(
        functools.partial(share_kernel, share, line),
        (1,),
        [scalars] + [whole(f.shape) for f in features],
        [whole(x) for x in shapes],
        [pltpu.HBM(x, bf16) for x in shapes],
        flops=6 * n_y * n_z * line * feat * clips,
    )(at, *features)


def unit_kernel(t_ref, emb_ref, all_ref, unit_ref, rows_ref, cols_ref, own_ref):
    parts, _, own, quarter = emb_ref.shape
    for m in range(3):
        emb = jnp.concatenate([emb_ref[e, m] for e in range(parts)], axis=1)
        values = emb.astype(f32)
        length = jnp.sqrt(jnp.sum(values * values, axis=1, keepdims=True) + epsilon)
        unit = (values / length).astype(bf16)
        all_ref[m] = emb
        unit_ref[m] = unit
        if m > 0:
            cols_ref[m - 1] = unit
        if m < 2:
            for copy in range(rows_ref.shape[0]):
                rows_ref[copy, m] = unit
    total = jnp.zeros((1, parts * quarter), f32)
    for p, (a, b) in enumerate(couples):
        product = unit_ref[a].astype(f32) * unit_ref[b].astype(f32)
        total += t_ref[p] * jnp.sum(product, axis=0, keepdims=True)
    own_ref[...] = jnp.broadcast_to(jnp.sum(total, axis=1, keepdims=True), own_ref.shape)


def units(t, emb, copies):
    parts, _, own, quarter = emb.shape
    full = (3, own, parts * quarter)
    shapes = [full, full, (copies, 2, *full[1:]), (2, *full[1:])]
    return call(
        unit_kernel,
        (1,),
        [scalars, whole(emb.shape)],
        [whole(x) for x in shapes] + [whole((8, LANES))],
        [pltpu.HBM(x, bf16) for x in shapes] + [jax.ShapeDtypeStruct((8, LANES), f32)],
        flops=10**6,
    )(t, emb)


def pair_scores(t_ref, rows_ref, cols_ref):
    own, width = rows_ref.shape[2], rows_ref.shape[3]
    rows = [rows_ref[:, m].reshape(rows_ref.shape[0] * own, width) for m in range(2)]
    cols = [cols_ref[:, m].reshape(cols_ref.shape[0] * own, width) for m in range(2)]
    shifted = []
    for p, (a, b) in enumerate(((0, 0), (0, 1), (1, 1))):
        t = t_ref[p]
        shifted.append(jnp.exp(t * contract(rows[a], cols[b], ((1,), (1,))) - t))
    return rows, cols, shifted


def score_kernel(t_ref, at_ref, rows_ref, cols_ref, own_ref, send_ref, keep_ref, row_ref, col_ref):
    step = pl.program_id(0)
    _, _, shifted = pair_scores(t_ref, rows_ref, cols_ref)
    rows = pl.ds(pl.multiple_of(step * TILE, TILE), TILE)

    @pl.when(step == 0)
    def _():
        col_ref[...] = jnp.zeros_like(col_ref)
        row_ref[...] = jnp.broadcast_to(own_ref[:, 0:1], row_ref.shape)

    for p, e in enumerate(shifted):
        col_ref[p : p + 1, :] += jnp.sum(e, axis=0, keepdims=True)
        total = jnp.broadcast_to(jnp.sum(e, axis=1, keepdims=True), (TILE, LANES))
        row_ref[p : p + 1, rows] = total.T[0:1]

    @pl.when(step == pl.num_programs(0) - 1)
    def _():
        first = at_ref[2] == 0
        send_ref[...] = jnp.where(first, row_ref[...], col_ref[...])
        keep_ref[...] = jnp.where(first, col_ref[...], row_ref[...])


def scores(t, at, rows, cols, own_scores):
    n_row, _, own, width = rows.shape
    block = n_row * own
    return call(
        score_kernel,
        (block // TILE,),
        [
            scalars,
            scalars,
            pl.BlockSpec((TILE // own, 2, own, width), lambda i: (i, 0, 0, 0)),
            whole(cols.shape),
            whole(own_scores.shape),
        ],
        [whole((8, block))] * 2,
        [jax.ShapeDtypeStruct((8, block), f32)] * 2,
        [pltpu.VMEM((8, block), f32)] * 2,
        flops=6 * block * block * width,
    )(t, at, rows, cols, own_scores)


def gather_kernel(at_ref, keep_ref, got_ref, out_ref):
    first = at_ref[2] == 0
    keep, got = keep_ref[...], got_ref[...]
    top = jnp.where(first, keep + got, got)[0:4]
    both = jnp.concatenate([top, keep[0:4]], axis=0)
    for copy in range(out_ref.shape[0]):
        out_ref[copy] = both


def sum_kernel(at_ref, both_ref, out_ref):
    first = at_ref[2] == 0
    out = jnp.zeros(out_ref.shape, f32)
    for i in range(both_ref.shape[0]):
        out += jnp.where(jnp.logical_and(first, at_ref[5] != i % 2), 0.0, both_ref[i])
    out_ref[...] = out


def small(kernel, at, arrays, shape):
    return call(
        kernel,
        (1,),
        [scalars] + [whole(x.shape) for x in arrays],
        whole(shape),
        jax.ShapeDtypeStruct(shape, f32),
        flops=10**5,
    )(at, *arrays)


def softmax_sums(at_ref, tot_ref, got_ref):
    first = at_ref[2] == 0
    row = jnp.where(first, got_ref[0:4], tot_ref[4:8])
    col = jnp.where(first, tot_ref[0:4], got_ref[0:4])
    return row, col


def product_kernel(
    t_ref, at_ref, rows_ref, cols_ref, tot_ref, got_ref, out_ref, keep_ref, send_ref, w_ref, hr_ref, hc_ref, acc_ref
):
    step = pl.program_id(0)
    per, _, own, width = rows_ref.shape
    block = cols_ref.shape[0] * own
    my_row, my_col, my_core = at_ref[0], at_ref[1], at_ref[2]

    @pl.when(step == 0)
    def _():
        row, col = softmax_sums(at_ref, tot_ref, got_ref)
        hc_ref[0:4, :] = 0.5 / col
        row = 0.5 / row
        for p in range(3):
            hr_ref[p] = jnp.broadcast_to(row[p : p + 1], (LANES, block)).T
            hr_ref[3] = jnp.broadcast_to(hc_ref[p : p + 1, :], (LANES, block)).T
            w_ref[p] = (
                hr_ref[p, pl.ds(pl.multiple_of(my_row * own, own), own), :]
                + hr_ref[3, pl.ds(pl.multiple_of(my_col * own, own), own), :]
            )

    rows, cols, shifted = pair_scores(t_ref, rows_ref, cols_ref)
    row_id = lax.broadcasted_iota(jnp.int32, (TILE, block), 0) + (step * TILE - my_row * own)
    col_id = lax.broadcasted_iota(jnp.int32, (TILE, block), 1) - my_col * own
    own_term = (row_id == col_id) & (row_id >= 0) & (row_id < own)
    grads = []
    for p in range(3):
        half = hr_ref[p, pl.ds(pl.multiple_of(step * TILE, TILE), TILE), :]
        half = jnp.concatenate([half] * (block // LANES), axis=1)
        g = shifted[p] * (half + hc_ref[p : p + 1, :])
        grads.append(jnp.where(own_term, 0.0, g).astype(bf16))
    d0 = t_ref[0] * contract(grads[0], cols[0], ((1,), (0,)))
    d0 += t_ref[1] * contract(grads[1], cols[1], ((1,), (0,)))
    d1 = t_ref[2] * contract(grads[2], cols[1], ((1,), (0,)))
    out_ref[:, 0] = d0.astype(bf16).reshape(per, own, width)
    out_ref[:, 1] = d1.astype(bf16).reshape(per, own, width)
    d1 = t_ref[0] * contract(grads[0], rows[0], ((0,), (0,)))
    d2 = t_ref[1] * contract(grads[1], rows[0], ((0,), (0,)))
    d2 += t_ref[2] * contract(grads[2], rows[1], ((0,), (0,)))
    last = pl.num_programs(0) - 1

    @pl.when(step == 0)
    def _():
        acc_ref[0] = d1
        acc_ref[1] = d2

    @pl.when((step > 0) & (step < last))
    def _():
        acc_ref[0] += d1
        acc_ref[1] += d2

    @pl.when(step == last)
    def _():
        for m, d in enumerate((d1, d2)):
            d = d + acc_ref[m]
            for i in range(block // (2 * own)):
                low = d[2 * i * own : (2 * i + 1) * own]
                high = d[(2 * i + 1) * own : (2 * i + 2) * own]
                keep_ref[i, m] = jnp.where(my_core == 0, low, high)
                send_ref[i, m] = jnp.where(my_core == 0, high, low).astype(bf16)


def products(t, at, rows, cols, tot, got):
    n_row, _, own, width = rows.shape
    block = n_row * own
    half = (block // own // 2, 2, own, width)
    tile = pl.BlockSpec((TILE // own, 2, own, width), lambda i: (i, 0, 0, 0))
    return call(
        product_kernel,
        (block // TILE,),
        [scalars, scalars, tile] + [whole(x.shape) for x in (cols, tot, got)],
        [tile, whole(half), whole(half), whole((3, own, LANES))],
        [
            pltpu.HBM(rows.shape, bf16),
            jax.ShapeDtypeStruct(half, f32),
            jax.ShapeDtypeStruct(half, bf16),
            jax.ShapeDtypeStruct((3, own, LANES), f32),
        ],
        [
            pltpu.VMEM((4, block, LANES), f32),
            pltpu.VMEM((8, block), f32),
            pltpu.VMEM((2, block, width), f32),
        ],
        flops=18 * block * block * width,
    )(t, at, rows, cols, tot, got)


def exact_parts(value, rows):
    line = lax.broadcasted_iota(jnp.int32, (rows, value.shape[1]), 0)
    rest = jnp.broadcast_to(value, line.shape)
    out = jnp.zeros(line.shape, f32)
    for i in range(3):
        part = rest.astype(bf16).astype(f32)
        out = jnp.where(line == i, part, out)
        rest = rest - part
    return out


def embed_kernel(
    n_row, n_col, scale, t_ref, at_ref, rows_ref, cols_ref, emb_ref, unit_ref, w_ref, tot_ref, got_ref, out_ref
):
    copies, parts = out_ref.shape[0], out_ref.shape[1]
    own, width = emb_ref.shape[1], emb_ref.shape[2]
    quarter = width // parts
    sums = [jnp.zeros((own, width), f32) for _ in range(2)]
    for i in range(rows_ref.shape[0]):
        for m in range(2):
            sums[m] += rows_ref[i, m].astype(f32)
    d_unit = [sums[0], sums[1] + cols_ref[0].astype(f32), cols_ref[1].astype(f32)]
    unit = [unit_ref[m].astype(f32) for m in range(3)]
    for p, (a, b) in enumerate(couples):
        t = t_ref[p]
        score = t * jnp.sum(unit[a] * unit[b], axis=1, keepdims=True)
        g = (jnp.exp(score - t) * w_ref[p][:, 0:1] - 1.0).astype(bf16).astype(f32)
        d_unit[a] += (t * g) * unit[b]
        d_unit[b] += (t * g) * unit[a]
    for m in range(3):
        values = emb_ref[m].astype(f32)
        length = jnp.sqrt(jnp.sum(values * values, axis=1, keepdims=True) + epsilon)
        value = values / length
        inner = jnp.sum(value * d_unit[m], axis=1, keepdims=True)
        d = ((d_unit[m] - value * inner) / length).astype(bf16)
        for c in range(copies):
            for e in range(parts):
                out_ref[c, e, m * own : (m + 1) * own, :] = d[:, e * quarter : (e + 1) * quarter]
    row, col = softmax_sums(at_ref, tot_ref, got_ref)
    loss = -2.0 / n_row * row[3:4, 0:1]
    for p in range(3):
        for sums_of, count in ((row, n_row), (col, n_col)):
            lse = t_ref[p] + jnp.log(sums_of[p : p + 1])
            loss += jnp.sum(lse, axis=1, keepdims=True) * (1.0 / count)
    tail = exact_parts(jnp.broadcast_to(loss * scale, (1, quarter)), 16).astype(bf16)
    for c in range(copies):
        for e in range(parts):
            out_ref[c, e, 3 * own : 3 * own + 16, :] = tail


def embed_gradients(t, at, rows, cols, emb, unit, w, tot, got, copies, parts, total):
    _, own, width = emb.shape
    shape = (copies, parts, 3 * own + 16, width // parts)
    kernel = functools.partial(
        embed_kernel, tot.shape[1] // own, tot.shape[1] // own, 1.0 / (2 * total)
    )
    arrays = (rows, cols, emb, unit, w, tot, got)
    return call(
        kernel,
        (1,),
        [scalars, scalars] + [whole(x.shape) for x in arrays],
        whole(shape),
        jax.ShapeDtypeStruct(shape, bf16),
        flops=10**6,
    )(t, at, *arrays)


def head_kernel(share, line, at_ref, d_ref, own_ref, mine_ref, other_ref, out_ref):
    n_y = 1 + mine_ref.shape[0]
    my_core, my_y = at_ref[2], at_ref[3]
    n_far, height, quarter = out_ref.shape
    n_z = n_far // 2
    parts = d_ref.shape[0] // n_y
    own = (d_ref.shape[1] - 16) // 3
    clips = parts * own
    tail = jnp.sum(d_ref[:, 3 * own : 3 * own + 16, :].astype(f32), axis=0)
    loss = exact_parts(jnp.sum(tail, axis=0, keepdims=True), 8)[: height - 3 * share]
    totals = []
    for m in range(3):
        there = [
            d_ref[
                pl.ds(lax.rem(my_y + (n_y - step), n_y) * parts, parts), m * own : (m + 1) * own, :
            ].reshape(clips, quarter)
            for step in range(n_y)
        ]
        there = jnp.concatenate(there, axis=0)
        mine = [mine_ref[step, m] for step in range(n_y - 1)]
        other = [other_ref[step, m] for step in range(n_y - 1)]
        for x in range(2):
            here = [jnp.where(my_core == x, a, b) for a, b in zip(mine, other)]
            here = jnp.concatenate([own_ref[x, m]] + here, axis=1)
            totals.append(contract(here, there, ((1,), (0,))))
    for far in range(n_far):
        x, z = far // n_z, far % n_z
        piece = [totals[2 * m + x][z * line : z * line + share] for m in range(3)]
        out_ref[far] = jnp.concatenate(piece + [loss], axis=0).astype(bf16)


def head_gradients(at, d, own, mine, other, share, line):
    n_z = own.shape[2] // line
    quarter = d.shape[2]
    shape = (2 * n_z, -(-(3 * share + 3) // 16) * 16, quarter)
    return call(
        functools.partial(head_kernel, share, line),
        (1,),
        [scalars] + [whole(x.shape) for x in (d, own, mine, other)],
        whole(shape),
        jax.ShapeDtypeStruct(shape, bf16),
        flops=10**9,
    )(at, d, own, mine, other)


def summing_groups(n_y, n_x, n_z, n_l):
    ids = np.arange(n_y * n_x * n_z * n_l * 2).reshape(n_y, n_x, n_z, n_l, 2)
    over_z = ids[..., 0].reshape(n_y * n_x, n_z * n_l)
    over_plane = ids[..., 1].transpose(2, 0, 1, 3).reshape(n_z, n_y * n_x * n_l)
    return over_z.tolist() + over_plane.tolist()


def shards(f0, f1, f2, h0, h1, h2, sharpness):
    features, heads = (f0, f1, f2), (h0, h1, h2)
    clips, feat = f0.shape
    quarter = h0.shape[1]
    emb_size = lax.axis_size(EMB)
    n_y, n_x, n_z = lax.axis_size("y"), lax.axis_size("xh"), lax.axis_size("z")
    n_row = lax.axis_size(ROW)
    own = clips // emb_size
    block_r = n_row * own
    at = jnp.stack(
        [lax.axis_index(axes) for axes in (ROW, COL, "core", "y", "xh", "xl")]
    ).astype(jnp.int32)

    share = feat // n_y // n_x // n_z
    line = -(-share // 8) * 8
    swap = [(0, 1), (1, 0)]
    wide, *sent = feature_shares(at, features, n_y, n_z, line)
    sent = [
        lax.ppermute(piece, "y", [(i, (i + step) % n_y) for i in range(n_y)])
        for step, piece in enumerate(sent, 1)
    ]
    mine = jnp.stack(sent)
    other = lax.ppermute(mine, "core", swap)

    emb = jnp.stack(
        [contract(f, h, ((1,), (0,))).astype(bf16) for f, h in zip(features, heads)]
    )
    emb = emb.reshape(3, emb_size, own, quarter).transpose(1, 0, 2, 3)
    emb, unit, rows, cols, own_scores = units(sharpness, exchange(emb, EMB), n_row)

    cols = lax.all_gather(cols, COL, axis=0)
    rows = exchange(rows, ROW)
    rows, wide, mine, other = lax.optimization_barrier((rows, wide, mine, other))

    send, keep = scores(sharpness, at, rows, cols, own_scores)
    both = small(gather_kernel, at, (keep, lax.ppermute(send, "core", swap)), (n_row, 8, block_r))
    groups = summing_groups(n_y, n_x, n_z, 2)
    both = lax.all_to_all(
        both, ("y", "xh", "z", "xl", "core"), 0, 0, axis_index_groups=groups, tiled=True
    )
    tot = small(sum_kernel, at, (both,), (8, block_r))
    got = lax.ppermute(tot, "core", swap)

    d_rows, keep, send, w = products(sharpness, at, rows, cols, tot, got)
    received = lax.ppermute(send, "core", swap)
    d_cols = (keep + received.astype(f32)).astype(bf16)
    d_cols = lax.psum_scatter(d_cols, "z", scatter_dimension=0)
    d_rows = exchange(d_rows, ROW)

    d_emb = embed_gradients(
        sharpness, at, d_rows, d_cols, emb, unit, w, tot, got, n_y, emb_size, clips * lax.axis_size(DP)
    )
    d_emb = exchange(d_emb.reshape(n_y * emb_size, 3 * own + 16, quarter), NEAR)

    out = head_gradients(at, d_emb, wide, mine, other, share, line)
    out = jnp.sum(exchange(out, FAR).astype(f32), axis=0)
    loss = out[3 * share, 0] + out[3 * share + 1, 0] + out[3 * share + 2, 0]
    return loss, out[:share], out[share : 2 * share], out[2 * share : 3 * share]


def solution(mesh):
    fine = Mesh(mesh.devices.reshape(4, 2, 8, 2, 2), ("y", "xh", "z", "xl", "core"))
    clip_rows, columns = P(DP, None), P(None, EMB)
    out = P(DP, EMB)
    return jax.shard_map(
        shards,
        mesh=fine,
        in_specs=(clip_rows,) * 3 + (columns,) * 3 + (P(),),
        out_specs=(P(), out, out, out),
        check_vma=False,
    )
```

```python
import functools

import jax
import jax.numpy as jnp
import numpy as np
from jax import lax
from jax.experimental import pallas as pl
from jax.experimental.pallas import tpu as pltpu
from jax.sharding import Mesh, PartitionSpec as P

epsilon = 1e-06
couples = ((0, 1), (0, 2), (1, 2))
EMB = ("xl", "core")
DP = ("y", "xh", "z")
ROW = ("y", "xh", "xl")
COL = ("z", "core")
NEAR = ("y", "xl", "core")
FAR = ("xh", "z")
bf16 = jnp.bfloat16
f32 = jnp.float32
LANES = 128


def exchange(pieces, axes):
    return lax.all_to_all(pieces, axes, split_axis=0, concat_axis=0, tiled=True)


def spread(value, axes):
    count = lax.axis_size(axes)
    return exchange(jnp.broadcast_to(value[None], (count, *value.shape)), axes)


def contract(left, right, dims):
    return lax.dot_general(left, right, (dims, ((), ())), preferred_element_type=f32)


def call(kernel, grid, in_specs, out_specs, out_shape, scratch=(), flops=0, room=32):
    return pl.pallas_call(
        kernel,
        grid=grid,
        in_specs=in_specs,
        out_specs=out_specs,
        out_shape=out_shape,
        scratch_shapes=scratch,
        compiler_params=pltpu.CompilerParams(vmem_limit_bytes=room * 2**20),
        cost_estimate=pl.CostEstimate(flops=flops, bytes_accessed=8 * 2**20, transcendentals=0),
    )


def whole(shape):
    return pl.BlockSpec(shape, lambda *_: (0,) * len(shape))


scalars = pl.BlockSpec(memory_space=pltpu.SMEM)
remote = pl.BlockSpec(memory_space=pltpu.HBM)


def share_kernel(share, line, at_ref, f0_ref, f1_ref, f2_ref, own_ref, *send_refs):
    n_y = 1 + len(send_refs)
    rows, feat = own_ref.shape[2], f0_ref.shape[1]
    r = lax.broadcasted_iota(jnp.int32, (rows, 1), 0)
    place = r // line
    inside = r - place * line < share
    column = lax.broadcasted_iota(jnp.int32, (rows, feat), 1)
    jobs = [(own_ref.at[x], 0, x) for x in range(2)]
    jobs += [(ref, step, at_ref[2]) for step, ref in enumerate(send_refs, 1)]
    for ref, step, x in jobs:
        start = (2 * lax.rem(at_ref[3] + step, n_y) + x) * (feat // n_y // 2)
        target = jnp.where(inside, r - place * (line - share) + start, -1)
        pick = jnp.where(column == target, 1.0, 0.0).astype(bf16)
        for m, f_ref in enumerate((f0_ref, f1_ref, f2_ref)):
            ref[m] = contract(pick, f_ref[...], ((1,), (1,))).astype(bf16)


def feature_shares(at, features, n_y, n_z, line):
    clips, feat = features[0].shape
    share = feat // n_y // n_z // 2
    shape = (3, n_z * line, clips)
    shapes = [(2, *shape)] + [shape] * (n_y - 1)
    return call(
        functools.partial(share_kernel, share, line),
        (1,),
        [scalars] + [whole(f.shape) for f in features],
        [whole(x) for x in shapes],
        [pltpu.HBM(x, bf16) for x in shapes],
        flops=6 * n_y * n_z * line * feat * clips,
    )(at, *features)


def unit_kernel(t_ref, emb_ref, all_ref, unit_ref, rows_ref, cols_ref, own_ref):
    parts, _, own, quarter = emb_ref.shape
    for m in range(3):
        emb = jnp.concatenate([emb_ref[e, m] for e in range(parts)], axis=1)
        values = emb.astype(f32)
        length = jnp.sqrt(jnp.sum(values * values, axis=1, keepdims=True) + epsilon)
        unit = (values / length).astype(bf16)
        all_ref[m] = emb
        unit_ref[m] = unit
        if m > 0:
            cols_ref[m - 1] = unit
        if m < 2:
            for copy in range(rows_ref.shape[0]):
                rows_ref[copy, m] = unit
    total = jnp.zeros((1, parts * quarter), f32)
    for p, (a, b) in enumerate(couples):
        product = unit_ref[a].astype(f32) * unit_ref[b].astype(f32)
        total += t_ref[p] * jnp.sum(product, axis=0, keepdims=True)
    own_ref[...] = jnp.broadcast_to(jnp.sum(total, axis=1, keepdims=True), own_ref.shape)


def units(t, emb, copies):
    parts, _, own, quarter = emb.shape
    full = (3, own, parts * quarter)
    shapes = [full, full, (copies, 2, *full[1:]), (2, *full[1:])]
    return call(
        unit_kernel,
        (1,),
        [scalars, whole(emb.shape)],
        [whole(x) for x in shapes] + [whole((8, LANES))],
        [pltpu.HBM(x, bf16) for x in shapes] + [jax.ShapeDtypeStruct((8, LANES), f32)],
        flops=10**6,
    )(t, emb)


def far_memory(value):
    return pltpu.with_memory_space_constraint(value, pltpu.HBM)


def shifted_scores(t, rows, cols):
    return jnp.exp(t * contract(rows, cols, ((1,), (1,))) - t)


def score_kernel(t_ref, at_ref, rows_ref, cols_hbm, own_ref, send_ref, keep_ref, cols_ref, sems):
    n_row, _, own, width = rows_ref.shape
    block = n_row * own
    copies = [pltpu.make_async_copy(cols_hbm.at[:, m], cols_ref.at[m], sems.at[m]) for m in range(2)]
    for copy in copies:
        copy.start()
    rows = [rows_ref[:, m].reshape(block, width) for m in range(2)]
    row_sums, col_sums = [], []
    for p, (a, b) in enumerate(((0, 0), (0, 1), (1, 1))):
        if p < 2:
            copies[p].wait()
        e = shifted_scores(t_ref[p], rows[a], cols_ref[b].reshape(block, width))
        col_sums.append(jnp.sum(e, axis=0, keepdims=True))
        total = jnp.broadcast_to(jnp.sum(e, axis=1, keepdims=True), (block, LANES))
        row_sums.append(total.T[0:1])
    own_sum = jnp.broadcast_to(own_ref[:, 0:1], (8, block))
    row = jnp.concatenate(row_sums + [own_sum[0:5]], axis=0)
    col = jnp.concatenate(col_sums + [own_sum[0:5]], axis=0)
    first = at_ref[2] == 0
    send_ref[...] = jnp.where(first, row, col)
    keep_ref[...] = jnp.where(first, col, row)


def scores(t, at, rows, cols, own_scores):
    n_row, _, own, width = rows.shape
    block = n_row * own
    return call(
        score_kernel,
        (1,),
        [scalars, scalars, whole(rows.shape), remote, whole(own_scores.shape)],
        [whole((8, block))] * 2,
        [jax.ShapeDtypeStruct((8, block), f32)] * 2,
        [pltpu.VMEM((2, n_row, own, width), bf16), pltpu.SemaphoreType.DMA((2,))],
        flops=6 * block * block * width,
    )(t, at, rows, far_memory(cols), own_scores)


def gather_kernel(at_ref, keep_ref, got_ref, out_ref):
    first = at_ref[2] == 0
    keep, got = keep_ref[...], got_ref[...]
    top = jnp.where(first, keep + got, got)[0:4]
    both = jnp.concatenate([top, keep[0:4]], axis=0)
    for copy in range(out_ref.shape[0]):
        out_ref[copy] = both


def sum_kernel(at_ref, both_ref, out_ref):
    first = at_ref[2] == 0
    out = jnp.zeros(out_ref.shape, f32)
    for i in range(both_ref.shape[0]):
        out += jnp.where(jnp.logical_and(first, at_ref[5] != i % 2), 0.0, both_ref[i])
    out_ref[...] = out


def small(kernel, at, arrays, shape):
    return call(
        kernel,
        (1,),
        [scalars] + [whole(x.shape) for x in arrays],
        whole(shape),
        jax.ShapeDtypeStruct(shape, f32),
        flops=10**5,
    )(at, *arrays)


def softmax_sums(at_ref, tot_ref, got_ref):
    first = at_ref[2] == 0
    row = jnp.where(first, got_ref[0:4], tot_ref[4:8])
    col = jnp.where(first, tot_ref[0:4], got_ref[0:4])
    return row, col


def product_kernel(
    t_ref, at_ref, rows_ref, cols_ref, tot_ref, got_ref, out_hbm, keep_ref, send_ref, w_ref, hr_ref, out_ref, sems
):
    n_row, _, own, width = rows_ref.shape
    block = n_row * own
    my_row, my_col, my_core = at_ref[0], at_ref[1], at_ref[2]
    row, col = softmax_sums(at_ref, tot_ref, got_ref)
    row, col = 0.5 / row, 0.5 / col
    for p in range(3):
        hr_ref[p] = jnp.broadcast_to(row[p : p + 1], (LANES, block)).T
        hr_ref[3] = jnp.broadcast_to(col[p : p + 1], (LANES, block)).T
        w_ref[p] = (
            hr_ref[p, pl.ds(pl.multiple_of(my_row * own, own), own), :]
            + hr_ref[3, pl.ds(pl.multiple_of(my_col * own, own), own), :]
        )

    rows = [rows_ref[:, m].reshape(block, width) for m in range(2)]
    cols = [cols_ref[:, m].reshape(block, width) for m in range(2)]
    row_id = lax.broadcasted_iota(jnp.int32, (block, block), 0) - my_row * own
    col_id = lax.broadcasted_iota(jnp.int32, (block, block), 1) - my_col * own
    own_term = (row_id == col_id) & (row_id >= 0) & (row_id < own)
    grads = []
    for p, (a, b) in enumerate(((0, 0), (0, 1), (1, 1))):
        half = jnp.concatenate([hr_ref[p]] * (block // LANES), axis=1)
        g = shifted_scores(t_ref[p], rows[a], cols[b]) * (half + col[p : p + 1])
        grads.append(jnp.where(own_term, 0.0, g).astype(bf16))
    d0 = t_ref[0] * contract(grads[0], cols[0], ((1,), (0,)))
    d0 += t_ref[1] * contract(grads[1], cols[1], ((1,), (0,)))
    d1 = t_ref[2] * contract(grads[2], cols[1], ((1,), (0,)))
    copies = []
    for m, d in enumerate((d0, d1)):
        out_ref[m] = d.astype(bf16).reshape(n_row, own, width)
        copies.append(pltpu.make_async_copy(out_ref.at[m], out_hbm.at[:, m], sems.at[m]))
        copies[m].start()
    d1 = t_ref[0] * contract(grads[0], rows[0], ((0,), (0,)))
    d2 = t_ref[1] * contract(grads[1], rows[0], ((0,), (0,)))
    d2 += t_ref[2] * contract(grads[2], rows[1], ((0,), (0,)))
    for m, d in enumerate((d1, d2)):
        for i in range(block // (2 * own)):
            low = d[2 * i * own : (2 * i + 1) * own]
            high = d[(2 * i + 1) * own : (2 * i + 2) * own]
            keep_ref[i, m] = jnp.where(my_core == 0, low, high).astype(bf16)
            send_ref[i, m] = jnp.where(my_core == 0, high, low).astype(bf16)
    for copy in copies:
        copy.wait()


def products(t, at, rows, cols, tot, got):
    n_row, _, own, width = rows.shape
    block = n_row * own
    half = (n_row // 2, 2, own, width)
    return call(
        product_kernel,
        (1,),
        [scalars, scalars] + [whole(x.shape) for x in (rows, cols, tot, got)],
        [remote, whole(half), whole(half), whole((3, own, LANES))],
        [
            pltpu.HBM(rows.shape, bf16),
            jax.ShapeDtypeStruct(half, bf16),
            jax.ShapeDtypeStruct(half, bf16),
            jax.ShapeDtypeStruct((3, own, LANES), f32),
        ],
        [
            pltpu.VMEM((4, block, LANES), f32),
            pltpu.VMEM((2, n_row, own, width), bf16),
            pltpu.SemaphoreType.DMA((2,)),
        ],
        flops=18 * block * block * width,
    )(t, at, rows, cols, tot, got)


def exact_parts(value, rows):
    line = lax.broadcasted_iota(jnp.int32, (rows, value.shape[1]), 0)
    rest = jnp.broadcast_to(value, line.shape)
    out = jnp.zeros(line.shape, f32)
    for i in range(3):
        part = rest.astype(bf16).astype(f32)
        out = jnp.where(line == i, part, out)
        rest = rest - part
    return out


def embed_kernel(
    n_row, n_col, scale, t_ref, at_ref, rows_ref, cols_hbm, emb_hbm, unit_hbm, w_ref, tot_ref, got_ref, out_ref, cols_ref, emb_ref, unit_ref, sems
):
    pairs = ((cols_hbm, cols_ref), (emb_hbm, emb_ref), (unit_hbm, unit_ref))
    loads = [pltpu.make_async_copy(*pair, sems.at[i]) for i, pair in enumerate(pairs)]
    for load in loads:
        load.start()
    copies, parts = out_ref.shape[0], out_ref.shape[1]
    own, width = emb_ref.shape[1], emb_ref.shape[2]
    quarter = width // parts
    sums = [jnp.zeros((own, width), f32) for _ in range(2)]
    for i in range(rows_ref.shape[0]):
        for m in range(2):
            sums[m] += rows_ref[i, m].astype(f32)
    for load in loads:
        load.wait()
    d_unit = [sums[0], sums[1] + cols_ref[0].astype(f32), cols_ref[1].astype(f32)]
    unit = [unit_ref[m].astype(f32) for m in range(3)]
    for p, (a, b) in enumerate(couples):
        t = t_ref[p]
        score = t * jnp.sum(unit[a] * unit[b], axis=1, keepdims=True)
        g = (jnp.exp(score - t) * w_ref[p][:, 0:1] - 1.0).astype(bf16).astype(f32)
        d_unit[a] += (t * g) * unit[b]
        d_unit[b] += (t * g) * unit[a]
    for m in range(3):
        values = emb_ref[m].astype(f32)
        length = jnp.sqrt(jnp.sum(values * values, axis=1, keepdims=True) + epsilon)
        value = values / length
        inner = jnp.sum(value * d_unit[m], axis=1, keepdims=True)
        d = ((d_unit[m] - value * inner) / length).astype(bf16)
        for c in range(copies):
            for e in range(parts):
                out_ref[c, e, m * own : (m + 1) * own, :] = d[:, e * quarter : (e + 1) * quarter]
    row, col = softmax_sums(at_ref, tot_ref, got_ref)
    loss = -2.0 / n_row * row[3:4, 0:1]
    for p in range(3):
        for sums_of, count in ((row, n_row), (col, n_col)):
            lse = t_ref[p] + jnp.log(sums_of[p : p + 1])
            loss += jnp.sum(lse, axis=1, keepdims=True) * (1.0 / count)
    tail = exact_parts(jnp.broadcast_to(loss * scale, (1, quarter)), 16).astype(bf16)
    for c in range(copies):
        for e in range(parts):
            out_ref[c, e, 3 * own : 3 * own + 16, :] = tail


def embed_gradients(t, at, rows, cols, emb, unit, w, tot, got, copies, parts, total):
    _, own, width = emb.shape
    shape = (copies, parts, 3 * own + 16, width // parts)
    kernel = functools.partial(
        embed_kernel, tot.shape[1] // own, tot.shape[1] // own, 1.0 / (2 * total)
    )
    arrays = (rows, far_memory(cols), far_memory(emb), far_memory(unit), w, tot, got)
    return call(
        kernel,
        (1,),
        [scalars, scalars, whole(rows.shape)] + [remote] * 3 + [whole(x.shape) for x in (w, tot, got)],
        whole(shape),
        jax.ShapeDtypeStruct(shape, bf16),
        [pltpu.VMEM(x.shape, bf16) for x in (cols, emb, unit)] + [pltpu.SemaphoreType.DMA((3,))],
        flops=10**6,
    )(t, at, *arrays)


def head_kernel(share, line, at_ref, d_ref, own_ref, mine_ref, other_ref, out_ref):
    n_y = 1 + mine_ref.shape[0]
    my_core, my_y = at_ref[2], at_ref[3]
    n_far, height, quarter = out_ref.shape
    n_z = n_far // 2
    parts = d_ref.shape[0] // n_y
    own = (d_ref.shape[1] - 16) // 3
    clips = parts * own
    tail = jnp.sum(d_ref[:, 3 * own : 3 * own + 16, :].astype(f32), axis=0)
    loss = exact_parts(jnp.sum(tail, axis=0, keepdims=True), 8)[: height - 3 * share]
    totals = []
    for m in range(3):
        there = [
            d_ref[
                pl.ds(lax.rem(my_y + (n_y - step), n_y) * parts, parts), m * own : (m + 1) * own, :
            ].reshape(clips, quarter)
            for step in range(n_y)
        ]
        there = jnp.concatenate(there, axis=0)
        mine = [mine_ref[step, m] for step in range(n_y - 1)]
        other = [other_ref[step, m] for step in range(n_y - 1)]
        for x in range(2):
            here = [jnp.where(my_core == x, a, b) for a, b in zip(mine, other)]
            here = jnp.concatenate([own_ref[x, m]] + here, axis=1)
            totals.append(contract(here, there, ((1,), (0,))))
    for far in range(n_far):
        x, z = far // n_z, far % n_z
        piece = [totals[2 * m + x][z * line : z * line + share] for m in range(3)]
        out_ref[far] = jnp.concatenate(piece + [loss], axis=0).astype(bf16)


def head_gradients(at, d, own, mine, other, share, line):
    n_z = own.shape[2] // line
    quarter = d.shape[2]
    shape = (2 * n_z, -(-(3 * share + 3) // 16) * 16, quarter)
    return call(
        functools.partial(head_kernel, share, line),
        (1,),
        [scalars] + [whole(x.shape) for x in (d, own, mine, other)],
        whole(shape),
        jax.ShapeDtypeStruct(shape, bf16),
        flops=10**9,
    )(at, d, own, mine, far_memory(other))


def summing_groups(n_y, n_x, n_z, n_l):
    ids = np.arange(n_y * n_x * n_z * n_l * 2).reshape(n_y, n_x, n_z, n_l, 2)
    over_z = ids[..., 0].reshape(n_y * n_x, n_z * n_l)
    over_plane = ids[..., 1].transpose(2, 0, 1, 3).reshape(n_z, n_y * n_x * n_l)
    return over_z.tolist() + over_plane.tolist()


def shards(f0, f1, f2, h0, h1, h2, sharpness):
    features, heads = (f0, f1, f2), (h0, h1, h2)
    clips, feat = f0.shape
    quarter = h0.shape[1]
    emb_size = lax.axis_size(EMB)
    n_y, n_x, n_z = lax.axis_size("y"), lax.axis_size("xh"), lax.axis_size("z")
    n_row = lax.axis_size(ROW)
    own = clips // emb_size
    block_r = n_row * own
    at = jnp.stack(
        [lax.axis_index(axes) for axes in (ROW, COL, "core", "y", "xh", "xl")]
    ).astype(jnp.int32)

    share = feat // n_y // n_x // n_z
    line = -(-share // 8) * 8
    swap = [(0, 1), (1, 0)]
    wide, *sent = feature_shares(at, features, n_y, n_z, line)
    sent = [
        lax.ppermute(piece, "y", [(i, (i + step) % n_y) for i in range(n_y)])
        for step, piece in enumerate(sent, 1)
    ]
    mine = jnp.stack(sent)

    emb = jnp.stack(
        [contract(f, h, ((1,), (0,))).astype(bf16) for f, h in zip(features, heads)]
    )
    emb = emb.reshape(3, emb_size, own, quarter).transpose(1, 0, 2, 3)
    emb, unit, rows, cols, own_scores = units(sharpness, exchange(emb, EMB), n_row)

    cols = lax.all_gather(cols, COL, axis=0)
    rows = exchange(rows, ROW)
    other = lax.ppermute(mine, "core", swap)
    rows, wide, mine, other = lax.optimization_barrier((rows, wide, mine, other))

    send, keep = scores(sharpness, at, rows, cols, own_scores)
    both = small(gather_kernel, at, (keep, lax.ppermute(send, "core", swap)), (n_row, 8, block_r))
    groups = summing_groups(n_y, n_x, n_z, 2)
    both = lax.all_to_all(
        both, ("y", "xh", "z", "xl", "core"), 0, 0, axis_index_groups=groups, tiled=True
    )
    tot = small(sum_kernel, at, (both,), (8, block_r))
    got = lax.ppermute(tot, "core", swap)

    d_rows, keep, send, w = products(sharpness, at, rows, cols, tot, got)
    received = lax.ppermute(send, "core", swap)
    d_cols = (keep.astype(f32) + received.astype(f32)).astype(bf16)
    d_cols = lax.psum_scatter(d_cols, "z", scatter_dimension=0)
    d_rows = exchange(d_rows, ROW)

    d_emb = embed_gradients(
        sharpness, at, d_rows, d_cols, emb, unit, w, tot, got, n_y, emb_size, clips * lax.axis_size(DP)
    )
    d_emb = exchange(d_emb.reshape(n_y * emb_size, 3 * own + 16, quarter), NEAR)

    out = head_gradients(at, d_emb, wide, mine, other, share, line)
    out = jnp.sum(exchange(out, FAR).astype(f32), axis=0)
    loss = out[3 * share, 0] + out[3 * share + 1, 0] + out[3 * share + 2, 0]
    return loss, out[:share], out[share : 2 * share], out[2 * share : 3 * share]


def solution(mesh):
    fine = Mesh(mesh.devices.reshape(4, 2, 8, 2, 2), ("y", "xh", "z", "xl", "core"))
    clip_rows, columns = P(DP, None), P(None, EMB)
    out = P(DP, EMB)
    return jax.shard_map(
        shards,
        mesh=fine,
        in_specs=(clip_rows,) * 3 + (columns,) * 3 + (P(),),
        out_specs=(P(), out, out, out),
        check_vma=False,
    )
```

```python
import functools

import jax
import jax.numpy as jnp
import numpy as np
from jax import lax
from jax.experimental import pallas as pl
from jax.experimental.pallas import tpu as pltpu
from jax.sharding import Mesh, PartitionSpec as P

epsilon = 1e-06
couples = ((0, 1), (0, 2), (1, 2))
EMB = ("xl", "core")
DP = ("y", "xh", "z")
ROW = ("y", "xh", "xl")
COL = ("z", "core")
NEAR = ("y", "xl", "core")
FAR = ("xh", "z")
bf16 = jnp.bfloat16
f32 = jnp.float32
LANES = 128


def exchange(pieces, axes):
    return lax.all_to_all(pieces, axes, split_axis=0, concat_axis=0, tiled=True)


def contract(left, right, dims):
    return lax.dot_general(left, right, (dims, ((), ())), preferred_element_type=f32)


def call(kernel, grid, in_specs, out_specs, out_shape, scratch=(), flops=0, room=32):
    return pl.pallas_call(
        kernel,
        grid=grid,
        in_specs=in_specs,
        out_specs=out_specs,
        out_shape=out_shape,
        scratch_shapes=scratch,
        compiler_params=pltpu.CompilerParams(vmem_limit_bytes=room * 2**20),
        cost_estimate=pl.CostEstimate(flops=flops, bytes_accessed=8 * 2**20, transcendentals=0),
    )


def whole(shape):
    return pl.BlockSpec(shape, lambda *_: (0,) * len(shape))


scalars = pl.BlockSpec(memory_space=pltpu.SMEM)
remote = pl.BlockSpec(memory_space=pltpu.HBM)


def share_kernel(share, line, at_ref, f0_ref, f1_ref, f2_ref, own_ref, *send_refs):
    n_y = 1 + len(send_refs)
    rows, feat = own_ref.shape[2], f0_ref.shape[1]
    r = lax.broadcasted_iota(jnp.int32, (rows, 1), 0)
    place = r // line
    inside = r - place * line < share
    column = lax.broadcasted_iota(jnp.int32, (rows, feat), 1)
    jobs = [(own_ref.at[x], 0, x) for x in range(2)]
    jobs += [(ref, step, at_ref[2]) for step, ref in enumerate(send_refs, 1)]
    for ref, step, x in jobs:
        start = (2 * lax.rem(at_ref[3] + step, n_y) + x) * (feat // n_y // 2)
        target = jnp.where(inside, r - place * (line - share) + start, -1)
        pick = jnp.where(column == target, 1.0, 0.0).astype(bf16)
        for m, f_ref in enumerate((f0_ref, f1_ref, f2_ref)):
            ref[m] = contract(pick, f_ref[...], ((1,), (1,))).astype(bf16)


def feature_shares(at, features, n_y, n_z, line):
    clips, feat = features[0].shape
    share = feat // n_y // n_z // 2
    shape = (3, n_z * line, clips)
    shapes = [(2, *shape)] + [shape] * (n_y - 1)
    return call(
        functools.partial(share_kernel, share, line),
        (1,),
        [scalars] + [whole(f.shape) for f in features],
        [whole(x) for x in shapes],
        [pltpu.HBM(x, bf16) for x in shapes],
        flops=6 * n_y * n_z * line * feat * clips,
    )(at, *features)


def project_kernel(*refs):
    out_ref = refs[6]
    parts, _, own, quarter = out_ref.shape
    for m in range(3):
        emb = contract(refs[m][...], refs[3 + m][...], ((1,), (0,))).astype(bf16)
        out_ref[:, m] = emb.reshape(parts, own, quarter)


def project(features, heads, parts):
    clips, quarter = features[0].shape[0], heads[0].shape[1]
    shape = (parts, 3, clips // parts, quarter)
    return call(
        project_kernel,
        (1,),
        [whole(x.shape) for x in features + heads],
        whole(shape),
        jax.ShapeDtypeStruct(shape, bf16),
        flops=10**8,
    )(*[far_memory(x) for x in features + heads])


def unit_kernel(t_ref, emb_ref, all_ref, unit_ref, rows_ref, cols_ref, own_ref):
    parts, _, own, quarter = emb_ref.shape
    for m in range(3):
        emb = jnp.concatenate([emb_ref[e, m] for e in range(parts)], axis=1)
        values = emb.astype(f32)
        length = jnp.sqrt(jnp.sum(values * values, axis=1, keepdims=True) + epsilon)
        unit = (values / length).astype(bf16)
        all_ref[m] = emb
        unit_ref[m] = unit
        if m > 0:
            cols_ref[m - 1] = unit
        if m < 2:
            for copy in range(rows_ref.shape[0]):
                rows_ref[copy, m] = unit
    total = jnp.zeros((1, parts * quarter), f32)
    for p, (a, b) in enumerate(couples):
        product = unit_ref[a].astype(f32) * unit_ref[b].astype(f32)
        total += t_ref[p] * jnp.sum(product, axis=0, keepdims=True)
    own_ref[...] = jnp.broadcast_to(jnp.sum(total, axis=1, keepdims=True), own_ref.shape)


def units(t, emb, copies):
    parts, _, own, quarter = emb.shape
    full = (3, own, parts * quarter)
    shapes = [full, full, (copies, 2, *full[1:]), (2, *full[1:])]
    return call(
        unit_kernel,
        (1,),
        [scalars, whole(emb.shape)],
        [whole(x) for x in shapes] + [whole((8, LANES))],
        [pltpu.HBM(x, bf16) for x in shapes] + [jax.ShapeDtypeStruct((8, LANES), f32)],
        flops=10**6,
    )(t, emb)


def far_memory(value):
    return pltpu.with_memory_space_constraint(value, pltpu.HBM)


def shifted_scores(t, rows, cols):
    return jnp.exp(t * contract(rows, cols, ((1,), (1,))) - t)


def score_kernel(t_ref, at_ref, rows_ref, cols_hbm, own_ref, send_ref, keep_ref, cols_ref, sems):
    n_row, _, own, width = rows_ref.shape
    block = n_row * own
    copies = [pltpu.make_async_copy(cols_hbm.at[:, m], cols_ref.at[m], sems.at[m]) for m in range(2)]
    for copy in copies:
        copy.start()
    rows = [rows_ref[:, m].reshape(block, width) for m in range(2)]
    row_sums, col_sums = [], []
    for p, (a, b) in enumerate(((0, 0), (0, 1), (1, 1))):
        if p < 2:
            copies[p].wait()
        e = shifted_scores(t_ref[p], rows[a], cols_ref[b].reshape(block, width))
        col_sums.append(jnp.sum(e, axis=0, keepdims=True))
        total = jnp.broadcast_to(jnp.sum(e, axis=1, keepdims=True), (block, LANES))
        row_sums.append(total.T[0:1])
    own_sum = jnp.broadcast_to(own_ref[:, 0:1], (8, block))
    row = jnp.concatenate(row_sums + [own_sum[0:5]], axis=0)
    col = jnp.concatenate(col_sums + [own_sum[0:5]], axis=0)
    first = at_ref[2] == 0
    send_ref[...] = jnp.where(first, row, col)
    keep_ref[...] = jnp.where(first, col, row)


def scores(t, at, rows, cols, own_scores):
    n_row, _, own, width = rows.shape
    block = n_row * own
    return call(
        score_kernel,
        (1,),
        [scalars, scalars, whole(rows.shape), remote, whole(own_scores.shape)],
        [whole((8, block))] * 2,
        [jax.ShapeDtypeStruct((8, block), f32)] * 2,
        [pltpu.VMEM((2, n_row, own, width), bf16), pltpu.SemaphoreType.DMA((2,))],
        flops=6 * block * block * width,
    )(t, at, rows, far_memory(cols), own_scores)


def gather_kernel(at_ref, keep_ref, got_ref, out_ref):
    first = at_ref[2] == 0
    keep, got = keep_ref[...], got_ref[...]
    top = jnp.where(first, keep + got, got)[0:4]
    both = jnp.concatenate([top, keep[0:4]], axis=0)
    for copy in range(out_ref.shape[0]):
        out_ref[copy] = both


def sum_kernel(at_ref, both_ref, out_ref):
    first = at_ref[2] == 0
    out = jnp.zeros(out_ref.shape, f32)
    for i in range(both_ref.shape[0]):
        out += jnp.where(jnp.logical_and(first, at_ref[5] != i % 2), 0.0, both_ref[i])
    out_ref[...] = out


def small(kernel, at, arrays, shape):
    return call(
        kernel,
        (1,),
        [scalars] + [whole(x.shape) for x in arrays],
        whole(shape),
        jax.ShapeDtypeStruct(shape, f32),
        flops=10**5,
    )(at, *arrays)


def softmax_sums(at_ref, tot_ref, got_ref):
    first = at_ref[2] == 0
    row = jnp.where(first, got_ref[0:4], tot_ref[4:8])
    col = jnp.where(first, tot_ref[0:4], got_ref[0:4])
    return row, col


def product_kernel(
    t_ref, at_ref, rows_ref, cols_ref, tot_ref, got_ref, out_hbm, keep_ref, send_ref, w_ref, hr_ref, out_ref, sems
):
    n_row, _, own, width = rows_ref.shape
    block = n_row * own
    my_row, my_col, my_core = at_ref[0], at_ref[1], at_ref[2]
    row, col = softmax_sums(at_ref, tot_ref, got_ref)
    row, col = 0.5 / row, 0.5 / col
    for p in range(3):
        hr_ref[p] = jnp.broadcast_to(row[p : p + 1], (LANES, block)).T
        hr_ref[3] = jnp.broadcast_to(col[p : p + 1], (LANES, block)).T
        w_ref[p] = (
            hr_ref[p, pl.ds(pl.multiple_of(my_row * own, own), own), :]
            + hr_ref[3, pl.ds(pl.multiple_of(my_col * own, own), own), :]
        )

    rows = [rows_ref[:, m].reshape(block, width) for m in range(2)]
    cols = [cols_ref[:, m].reshape(block, width) for m in range(2)]
    row_id = lax.broadcasted_iota(jnp.int32, (block, block), 0) - my_row * own
    col_id = lax.broadcasted_iota(jnp.int32, (block, block), 1) - my_col * own
    own_term = (row_id == col_id) & (row_id >= 0) & (row_id < own)
    grads = []
    for p, (a, b) in enumerate(((0, 0), (0, 1), (1, 1))):
        half = jnp.concatenate([hr_ref[p]] * (block // LANES), axis=1)
        g = shifted_scores(t_ref[p], rows[a], cols[b]) * (half + col[p : p + 1])
        grads.append(jnp.where(own_term, 0.0, g).astype(bf16))
    d0 = t_ref[0] * contract(grads[0], cols[0], ((1,), (0,)))
    d0 += t_ref[1] * contract(grads[1], cols[1], ((1,), (0,)))
    d1 = t_ref[2] * contract(grads[2], cols[1], ((1,), (0,)))
    copies = []
    for m, d in enumerate((d0, d1)):
        out_ref[m] = d.astype(bf16).reshape(n_row, own, width)
        copies.append(pltpu.make_async_copy(out_ref.at[m], out_hbm.at[:, m], sems.at[m]))
        copies[m].start()
    d1 = t_ref[0] * contract(grads[0], rows[0], ((0,), (0,)))
    d2 = t_ref[1] * contract(grads[1], rows[0], ((0,), (0,)))
    d2 += t_ref[2] * contract(grads[2], rows[1], ((0,), (0,)))
    for m, d in enumerate((d1, d2)):
        for i in range(block // (2 * own)):
            low = d[2 * i * own : (2 * i + 1) * own]
            high = d[(2 * i + 1) * own : (2 * i + 2) * own]
            keep_ref[i, m] = jnp.where(my_core == 0, low, high).astype(bf16)
            send_ref[i, m] = jnp.where(my_core == 0, high, low).astype(bf16)
    for copy in copies:
        copy.wait()


def products(t, at, rows, cols, tot, got):
    n_row, _, own, width = rows.shape
    block = n_row * own
    half = (n_row // 2, 2, own, width)
    return call(
        product_kernel,
        (1,),
        [scalars, scalars] + [whole(x.shape) for x in (rows, cols, tot, got)],
        [remote, whole(half), whole(half), whole((3, own, LANES))],
        [
            pltpu.HBM(rows.shape, bf16),
            jax.ShapeDtypeStruct(half, bf16),
            jax.ShapeDtypeStruct(half, bf16),
            jax.ShapeDtypeStruct((3, own, LANES), f32),
        ],
        [
            pltpu.VMEM((4, block, LANES), f32),
            pltpu.VMEM((2, n_row, own, width), bf16),
            pltpu.SemaphoreType.DMA((2,)),
        ],
        flops=18 * block * block * width,
    )(t, at, rows, cols, tot, got)


def exact_parts(value, rows):
    line = lax.broadcasted_iota(jnp.int32, (rows, value.shape[1]), 0)
    rest = jnp.broadcast_to(value, line.shape)
    out = jnp.zeros(line.shape, f32)
    for i in range(3):
        part = rest.astype(bf16).astype(f32)
        out = jnp.where(line == i, part, out)
        rest = rest - part
    return out


def embed_kernel(
    n_row, n_col, scale, t_ref, at_ref, rows_ref, cols_hbm, emb_hbm, unit_hbm, w_ref, tot_ref, got_ref, out_ref, cols_ref, emb_ref, unit_ref, sems
):
    pairs = ((cols_hbm, cols_ref), (emb_hbm, emb_ref), (unit_hbm, unit_ref))
    loads = [pltpu.make_async_copy(*pair, sems.at[i]) for i, pair in enumerate(pairs)]
    for load in loads:
        load.start()
    copies, parts = out_ref.shape[0], out_ref.shape[1]
    own, width = emb_ref.shape[1], emb_ref.shape[2]
    quarter = width // parts
    sums = [jnp.zeros((own, width), f32) for _ in range(2)]
    for i in range(rows_ref.shape[0]):
        for m in range(2):
            sums[m] += rows_ref[i, m].astype(f32)
    for load in loads:
        load.wait()
    d_unit = [sums[0], sums[1] + cols_ref[0].astype(f32), cols_ref[1].astype(f32)]
    unit = [unit_ref[m].astype(f32) for m in range(3)]
    for p, (a, b) in enumerate(couples):
        t = t_ref[p]
        score = t * jnp.sum(unit[a] * unit[b], axis=1, keepdims=True)
        g = (jnp.exp(score - t) * w_ref[p][:, 0:1] - 1.0).astype(bf16).astype(f32)
        d_unit[a] += (t * g) * unit[b]
        d_unit[b] += (t * g) * unit[a]
    for m in range(3):
        values = emb_ref[m].astype(f32)
        length = jnp.sqrt(jnp.sum(values * values, axis=1, keepdims=True) + epsilon)
        value = values / length
        inner = jnp.sum(value * d_unit[m], axis=1, keepdims=True)
        d = ((d_unit[m] - value * inner) / length).astype(bf16)
        for c in range(copies):
            for e in range(parts):
                out_ref[c, e, m * own : (m + 1) * own, :] = d[:, e * quarter : (e + 1) * quarter]
    row, col = softmax_sums(at_ref, tot_ref, got_ref)
    loss = -2.0 / n_row * row[3:4, 0:1]
    for p in range(3):
        for sums_of, count in ((row, n_row), (col, n_col)):
            lse = t_ref[p] + jnp.log(sums_of[p : p + 1])
            loss += jnp.sum(lse, axis=1, keepdims=True) * (1.0 / count)
    tail = exact_parts(jnp.broadcast_to(loss * scale, (1, quarter)), 16).astype(bf16)
    for c in range(copies):
        for e in range(parts):
            out_ref[c, e, 3 * own : 3 * own + 16, :] = tail


def embed_gradients(t, at, rows, cols, emb, unit, w, tot, got, copies, parts, total):
    _, own, width = emb.shape
    shape = (copies, parts, 3 * own + 16, width // parts)
    kernel = functools.partial(
        embed_kernel, tot.shape[1] // own, tot.shape[1] // own, 1.0 / (2 * total)
    )
    arrays = (rows, far_memory(cols), far_memory(emb), far_memory(unit), w, tot, got)
    return call(
        kernel,
        (1,),
        [scalars, scalars, whole(rows.shape)] + [remote] * 3 + [whole(x.shape) for x in (w, tot, got)],
        whole(shape),
        jax.ShapeDtypeStruct(shape, bf16),
        [pltpu.VMEM(x.shape, bf16) for x in (cols, emb, unit)] + [pltpu.SemaphoreType.DMA((3,))],
        flops=10**6,
    )(t, at, *arrays)


def head_kernel(share, line, at_ref, d_ref, own_ref, mine_ref, other_ref, out_ref):
    n_y = 1 + mine_ref.shape[0]
    my_core, my_y = at_ref[2], at_ref[3]
    n_far, height, quarter = out_ref.shape
    n_z = n_far // 2
    parts = d_ref.shape[0] // n_y
    own = (d_ref.shape[1] - 16) // 3
    clips = parts * own
    tail = jnp.sum(d_ref[:, 3 * own : 3 * own + 16, :].astype(f32), axis=0)
    loss = exact_parts(jnp.sum(tail, axis=0, keepdims=True), 8)[: height - 3 * share]
    totals = []
    for m in range(3):
        there = [
            d_ref[
                pl.ds(lax.rem(my_y + (n_y - step), n_y) * parts, parts), m * own : (m + 1) * own, :
            ].reshape(clips, quarter)
            for step in range(n_y)
        ]
        there = jnp.concatenate(there, axis=0)
        mine = [mine_ref[step, m] for step in range(n_y - 1)]
        other = [other_ref[step, m] for step in range(n_y - 1)]
        for x in range(2):
            here = [jnp.where(my_core == x, a, b) for a, b in zip(mine, other)]
            here = jnp.concatenate([own_ref[x, m]] + here, axis=1)
            totals.append(contract(here, there, ((1,), (0,))))
    for far in range(n_far):
        x, z = far // n_z, far % n_z
        piece = [totals[2 * m + x][z * line : z * line + share] for m in range(3)]
        out_ref[far] = jnp.concatenate(piece + [loss], axis=0).astype(bf16)


def head_gradients(at, d, own, mine, other, share, line):
    n_z = own.shape[2] // line
    quarter = d.shape[2]
    shape = (2 * n_z, -(-(3 * share + 3) // 16) * 16, quarter)
    return call(
        functools.partial(head_kernel, share, line),
        (1,),
        [scalars] + [whole(x.shape) for x in (d, own, mine, other)],
        whole(shape),
        jax.ShapeDtypeStruct(shape, bf16),
        flops=10**9,
    )(at, d, own, mine, far_memory(other))


def total_kernel(share, in_ref, loss_ref, *out_refs):
    total = jnp.zeros(in_ref.shape[1:], f32)
    for i in range(in_ref.shape[0]):
        total += in_ref[i].astype(f32)
    for m, ref in enumerate(out_refs):
        ref[...] = total[m * share : (m + 1) * share]
    loss = jnp.sum(total[3 * share : 3 * share + 3], axis=0, keepdims=True)
    loss_ref[...] = loss[:, 0:1]


def totals(pieces, share):
    shapes = [(1, 1)] + [(share, pieces.shape[2])] * 3
    return call(
        functools.partial(total_kernel, share),
        (1,),
        [whole(pieces.shape)],
        [whole(x) for x in shapes],
        [jax.ShapeDtypeStruct(x, f32) for x in shapes],
        flops=10**6,
    )(pieces)


def summing_groups(n_y, n_x, n_z, n_l):
    ids = np.arange(n_y * n_x * n_z * n_l * 2).reshape(n_y, n_x, n_z, n_l, 2)
    over_z = ids[..., 0].reshape(n_y * n_x, n_z * n_l)
    over_plane = ids[..., 1].transpose(2, 0, 1, 3).reshape(n_z, n_y * n_x * n_l)
    return over_z.tolist() + over_plane.tolist()


def shards(f0, f1, f2, h0, h1, h2, sharpness):
    features, heads = (f0, f1, f2), (h0, h1, h2)
    clips, feat = f0.shape
    quarter = h0.shape[1]
    emb_size = lax.axis_size(EMB)
    n_y, n_x, n_z = lax.axis_size("y"), lax.axis_size("xh"), lax.axis_size("z")
    n_row = lax.axis_size(ROW)
    own = clips // emb_size
    block_r = n_row * own
    at = jnp.stack(
        [lax.axis_index(axes) for axes in (ROW, COL, "core", "y", "xh", "xl")]
    ).astype(jnp.int32)

    share = feat // n_y // n_x // n_z
    line = -(-share // 8) * 8
    swap = [(0, 1), (1, 0)]
    wide, *sent = feature_shares(at, features, n_y, n_z, line)
    sent = [
        lax.ppermute(piece, "y", [(i, (i + step) % n_y) for i in range(n_y)])
        for step, piece in enumerate(sent, 1)
    ]
    mine = jnp.stack(sent)

    emb = project(features, heads, emb_size)
    emb, unit, rows, cols, own_scores = units(sharpness, exchange(emb, EMB), n_row)

    cols = lax.all_gather(cols, COL, axis=0)
    rows = exchange(rows, ROW)
    other = lax.ppermute(mine, "core", swap)
    rows, wide, mine, other = lax.optimization_barrier((rows, wide, mine, other))

    send, keep = scores(sharpness, at, rows, cols, own_scores)
    both = small(gather_kernel, at, (keep, lax.ppermute(send, "core", swap)), (n_row, 8, block_r))
    groups = summing_groups(n_y, n_x, n_z, 2)
    both = lax.all_to_all(
        both, ("y", "xh", "z", "xl", "core"), 0, 0, axis_index_groups=groups, tiled=True
    )
    tot = small(sum_kernel, at, (both,), (8, block_r))
    got = lax.ppermute(tot, "core", swap)

    d_rows, keep, send, w = products(sharpness, at, rows, cols, tot, got)
    received = lax.ppermute(send, "core", swap)
    d_cols = (keep.astype(f32) + received.astype(f32)).astype(bf16)
    d_cols = lax.psum_scatter(d_cols, "z", scatter_dimension=0)
    d_rows = exchange(d_rows, ROW)

    d_emb = embed_gradients(
        sharpness, at, d_rows, d_cols, emb, unit, w, tot, got, n_y, emb_size, clips * lax.axis_size(DP)
    )
    d_emb = exchange(d_emb.reshape(n_y * emb_size, 3 * own + 16, quarter), NEAR)

    out = head_gradients(at, d_emb, wide, mine, other, share, line)
    loss, *out = totals(exchange(out, FAR), share)
    return loss.reshape(()), *out


def solution(mesh):
    fine = Mesh(mesh.devices.reshape(4, 2, 8, 2, 2), ("y", "xh", "z", "xl", "core"))
    clip_rows, columns = P(DP, None), P(None, EMB)
    out = P(DP, EMB)
    return jax.shard_map(
        shards,
        mesh=fine,
        in_specs=(clip_rows,) * 3 + (columns,) * 3 + (P(),),
        out_specs=(P(), out, out, out),
        check_vma=False,
    )
```

```python
import functools

import jax
import jax.numpy as jnp
import numpy as np
from jax import lax
from jax.experimental import pallas as pl
from jax.experimental.pallas import tpu as pltpu
from jax.sharding import Mesh, PartitionSpec as P

epsilon = 1e-06
couples = ((0, 1), (0, 2), (1, 2))
EMB = ("xl", "core")
DP = ("y", "xh", "z")
ROW = ("y", "xh", "xl")
COL = ("z", "core")
NEAR = ("y", "xl", "core")
FAR = ("xh", "z")
bf16 = jnp.bfloat16
f32 = jnp.float32
LANES = 128


def exchange(pieces, axes):
    return lax.all_to_all(pieces, axes, split_axis=0, concat_axis=0, tiled=True)


def contract(left, right, dims):
    return lax.dot_general(left, right, (dims, ((), ())), preferred_element_type=f32)


def call(kernel, grid, in_specs, out_specs, out_shape, scratch=(), flops=0, room=32):
    return pl.pallas_call(
        kernel,
        grid=grid,
        in_specs=in_specs,
        out_specs=out_specs,
        out_shape=out_shape,
        scratch_shapes=scratch,
        compiler_params=pltpu.CompilerParams(vmem_limit_bytes=room * 2**20),
        cost_estimate=pl.CostEstimate(flops=flops, bytes_accessed=8 * 2**20, transcendentals=0),
    )


def whole(shape):
    return pl.BlockSpec(shape, lambda *_: (0,) * len(shape))


scalars = pl.BlockSpec(memory_space=pltpu.SMEM)
remote = pl.BlockSpec(memory_space=pltpu.HBM)


def share_kernel(share, line, at_ref, f0_ref, f1_ref, f2_ref, own_ref, *send_refs):
    n_y = 1 + len(send_refs)
    rows, feat = own_ref.shape[2], f0_ref.shape[1]
    r = lax.broadcasted_iota(jnp.int32, (rows, 1), 0)
    place = r // line
    inside = r - place * line < share
    column = lax.broadcasted_iota(jnp.int32, (rows, feat), 1)
    jobs = [(own_ref.at[x], 0, x) for x in range(2)]
    jobs += [(ref, step, at_ref[2]) for step, ref in enumerate(send_refs, 1)]
    for ref, step, x in jobs:
        start = (2 * lax.rem(at_ref[3] + step, n_y) + x) * (feat // n_y // 2)
        target = jnp.where(inside, r - place * (line - share) + start, -1)
        pick = jnp.where(column == target, 1.0, 0.0).astype(bf16)
        for m, f_ref in enumerate((f0_ref, f1_ref, f2_ref)):
            ref[m] = contract(pick, f_ref[...], ((1,), (1,))).astype(bf16)


def feature_shares(at, features, n_y, n_z, line):
    clips, feat = features[0].shape
    share = feat // n_y // n_z // 2
    shape = (3, n_z * line, clips)
    shapes = [(2, *shape)] + [shape] * (n_y - 1)
    return call(
        functools.partial(share_kernel, share, line),
        (1,),
        [scalars] + [whole(f.shape) for f in features],
        [whole(x) for x in shapes],
        [pltpu.HBM(x, bf16) for x in shapes],
        flops=6 * n_y * n_z * line * feat * clips,
    )(at, *features)


def project_kernel(*refs):
    arrays, out_ref, buffers, sems = refs[:6], refs[6], refs[7:13], refs[13]
    parts, _, own, quarter = out_ref.shape
    copies = [pltpu.make_async_copy(arrays[i], buffers[i], sems.at[i]) for i in range(6)]
    for m in range(3):
        copies[m].start()
        copies[3 + m].start()
    for m in range(3):
        copies[m].wait()
        copies[3 + m].wait()
        emb = contract(buffers[m][...], buffers[3 + m][...], ((1,), (0,))).astype(bf16)
        out_ref[:, m] = emb.reshape(parts, own, quarter)


def project(features, heads, parts):
    clips, quarter = features[0].shape[0], heads[0].shape[1]
    shape = (parts, 3, clips // parts, quarter)
    arrays = features + heads
    return call(
        project_kernel,
        (1,),
        [remote] * 6,
        whole(shape),
        jax.ShapeDtypeStruct(shape, bf16),
        [pltpu.VMEM(x.shape, bf16) for x in arrays] + [pltpu.SemaphoreType.DMA((6,))],
        flops=10**8,
    )(*[far_memory(x) for x in arrays])


def unit_kernel(t_ref, emb_ref, all_ref, unit_ref, cols_ref, rows_ref, own_ref):
    parts, _, own, quarter = emb_ref.shape
    units = []
    for m in range(3):
        emb = jnp.concatenate([emb_ref[e, m] for e in range(parts)], axis=1)
        values = emb.astype(f32)
        length = jnp.sqrt(jnp.sum(values * values, axis=1, keepdims=True) + epsilon)
        unit = (values / length).astype(bf16)
        all_ref[m] = emb
        unit_ref[m] = unit
        units.append(unit.astype(f32))
        if m > 0:
            cols_ref[m - 1] = unit
        if m < 2:
            rows_ref[m] = unit
    total = jnp.zeros((1, parts * quarter), f32)
    for p, (a, b) in enumerate(couples):
        total += t_ref[p] * jnp.sum(units[a] * units[b], axis=0, keepdims=True)
    own_ref[...] = jnp.broadcast_to(jnp.sum(total, axis=1, keepdims=True), own_ref.shape)


def units(t, emb):
    parts, _, own, quarter = emb.shape
    full = (3, own, parts * quarter)
    two = (2, *full[1:])
    return call(
        unit_kernel,
        (1,),
        [scalars, whole(emb.shape)],
        [whole(x) for x in (full, full, two, two, (8, LANES))],
        [pltpu.HBM(x, bf16) for x in (full, full, two)]
        + [jax.ShapeDtypeStruct(two, bf16), jax.ShapeDtypeStruct((8, LANES), f32)],
        flops=10**6,
    )(t, emb)


def copies_kernel(in_ref, out_ref):
    for i in range(out_ref.shape[0]):
        out_ref[i] = in_ref[...]


def copies_of(value, count):
    zeros = (0,) * value.ndim
    return call(
        copies_kernel,
        (2,),
        [whole(value.shape)],
        pl.BlockSpec((count // 2, *value.shape), lambda i: (i, *zeros)),
        pltpu.HBM((count, *value.shape), value.dtype),
        flops=10**6,
    )(value)


def far_memory(value):
    return pltpu.with_memory_space_constraint(value, pltpu.HBM)


def shifted_scores(t, rows, cols):
    return jnp.exp(t * contract(rows, cols, ((1,), (1,))) - t)


def score_kernel(t_ref, at_ref, rows_ref, cols_hbm, own_ref, send_ref, keep_ref, cols_ref, sems):
    n_row, _, own, width = rows_ref.shape
    block = n_row * own
    copies = [pltpu.make_async_copy(cols_hbm.at[:, m], cols_ref.at[m], sems.at[m]) for m in range(2)]
    for copy in copies:
        copy.start()
    rows = [rows_ref[:, m].reshape(block, width) for m in range(2)]
    row_sums, col_sums = [], []
    for p, (a, b) in enumerate(((0, 0), (0, 1), (1, 1))):
        if p < 2:
            copies[p].wait()
        e = shifted_scores(t_ref[p], rows[a], cols_ref[b].reshape(block, width))
        col_sums.append(jnp.sum(e, axis=0, keepdims=True))
        total = jnp.broadcast_to(jnp.sum(e, axis=1, keepdims=True), (block, LANES))
        row_sums.append(total.T[0:1])
    own_sum = jnp.broadcast_to(own_ref[:, 0:1], (8, block))
    row = jnp.concatenate(row_sums + [own_sum[0:5]], axis=0)
    col = jnp.concatenate(col_sums + [own_sum[0:5]], axis=0)
    first = at_ref[2] == 0
    send_ref[...] = jnp.where(first, row, col)
    keep_ref[...] = jnp.where(first, col, row)


def scores(t, at, rows, cols, own_scores):
    n_row, _, own, width = rows.shape
    block = n_row * own
    return call(
        score_kernel,
        (1,),
        [scalars, scalars, whole(rows.shape), remote, whole(own_scores.shape)],
        [whole((8, block))] * 2,
        [jax.ShapeDtypeStruct((8, block), f32)] * 2,
        [pltpu.VMEM((2, n_row, own, width), bf16), pltpu.SemaphoreType.DMA((2,))],
        flops=6 * block * block * width,
    )(t, at, rows, far_memory(cols), own_scores)


def gather_kernel(at_ref, keep_ref, got_ref, out_ref):
    first = at_ref[2] == 0
    keep, got = keep_ref[...], got_ref[...]
    top = jnp.where(first, keep + got, got)[0:4]
    both = jnp.concatenate([top, keep[0:4]], axis=0)
    for copy in range(out_ref.shape[0]):
        out_ref[copy] = both


def sum_kernel(at_ref, both_ref, out_ref):
    first = at_ref[2] == 0
    out = jnp.zeros(out_ref.shape, f32)
    for i in range(both_ref.shape[0]):
        out += jnp.where(jnp.logical_and(first, at_ref[5] != i % 2), 0.0, both_ref[i])
    out_ref[...] = out


def small(kernel, at, arrays, shape):
    return call(
        kernel,
        (1,),
        [scalars] + [whole(x.shape) for x in arrays],
        whole(shape),
        jax.ShapeDtypeStruct(shape, f32),
        flops=10**5,
    )(at, *arrays)


def softmax_sums(at_ref, tot_ref, got_ref):
    first = at_ref[2] == 0
    row = jnp.where(first, got_ref[0:4], tot_ref[4:8])
    col = jnp.where(first, tot_ref[0:4], got_ref[0:4])
    return row, col


def product_kernel(
    t_ref, at_ref, rows_ref, cols_ref, tot_ref, got_ref, g_ref, keep_ref, send_ref, w_ref, hr_ref
):
    n_row, _, own, width = rows_ref.shape
    block = n_row * own
    my_row, my_col, my_core = at_ref[0], at_ref[1], at_ref[2]
    row, col = softmax_sums(at_ref, tot_ref, got_ref)
    row, col = 0.5 / row, 0.5 / col
    for p in range(3):
        hr_ref[p] = jnp.broadcast_to(row[p : p + 1], (LANES, block)).T
        hr_ref[3] = jnp.broadcast_to(col[p : p + 1], (LANES, block)).T
        w_ref[p] = (
            hr_ref[p, pl.ds(pl.multiple_of(my_row * own, own), own), :]
            + hr_ref[3, pl.ds(pl.multiple_of(my_col * own, own), own), :]
        )

    rows = [rows_ref[:, m].reshape(block, width) for m in range(2)]
    cols = [cols_ref[:, m].reshape(block, width) for m in range(2)]
    row_id = lax.broadcasted_iota(jnp.int32, (block, block), 0) - my_row * own
    col_id = lax.broadcasted_iota(jnp.int32, (block, block), 1) - my_col * own
    own_term = (row_id == col_id) & (row_id >= 0) & (row_id < own)
    grads = []
    for p, (a, b) in enumerate(((0, 0), (0, 1), (1, 1))):
        half = jnp.concatenate([hr_ref[p]] * (block // LANES), axis=1)
        g = shifted_scores(t_ref[p], rows[a], cols[b]) * (half + col[p : p + 1])
        grads.append(jnp.where(own_term, 0.0, g).astype(bf16))
        g_ref[p] = grads[p]
    d1 = t_ref[0] * contract(grads[0], rows[0], ((0,), (0,)))
    d2 = t_ref[1] * contract(grads[1], rows[0], ((0,), (0,)))
    d2 += t_ref[2] * contract(grads[2], rows[1], ((0,), (0,)))
    for m, d in enumerate((d1, d2)):
        for i in range(block // (2 * own)):
            low = d[2 * i * own : (2 * i + 1) * own]
            high = d[(2 * i + 1) * own : (2 * i + 2) * own]
            keep_ref[i, m] = jnp.where(my_core == 0, low, high).astype(bf16)
            send_ref[i, m] = jnp.where(my_core == 0, high, low).astype(bf16)


def row_kernel(t_ref, g_ref, cols_ref, out_hbm, out_ref, sems):
    n_row, own, width = out_ref.shape[1:]
    cols = [cols_ref[:, m].reshape(cols_ref.shape[0] * own, width) for m in range(2)]
    d0 = t_ref[0] * contract(g_ref[0], cols[0], ((1,), (0,)))
    d0 += t_ref[1] * contract(g_ref[1], cols[1], ((1,), (0,)))
    copies = []
    for m in range(2):
        d = d0 if m == 0 else t_ref[2] * contract(g_ref[2], cols[1], ((1,), (0,)))
        out_ref[m] = d.astype(bf16).reshape(n_row, own, width)
        copies.append(pltpu.make_async_copy(out_ref.at[m], out_hbm.at[:, m], sems.at[m]))
        copies[m].start()
    for copy in copies:
        copy.wait()


def row_products(t, g, cols):
    n_row, _, own, width = cols.shape
    return call(
        row_kernel,
        (1,),
        [scalars, whole(g.shape), whole(cols.shape)],
        remote,
        pltpu.HBM(cols.shape, bf16),
        [pltpu.VMEM((2, n_row, own, width), bf16), pltpu.SemaphoreType.DMA((2,))],
        flops=6 * (n_row * own) ** 2 * width,
    )(t, g, cols)


def products(t, at, rows, cols, tot, got):
    n_row, _, own, width = rows.shape
    block = n_row * own
    half = (n_row // 2, 2, own, width)
    return call(
        product_kernel,
        (1,),
        [scalars, scalars] + [whole(x.shape) for x in (rows, cols, tot, got)],
        [whole((3, block, block)), whole(half), whole(half), whole((3, own, LANES))],
        [
            jax.ShapeDtypeStruct((3, block, block), bf16),
            jax.ShapeDtypeStruct(half, bf16),
            jax.ShapeDtypeStruct(half, bf16),
            jax.ShapeDtypeStruct((3, own, LANES), f32),
        ],
        [pltpu.VMEM((4, block, LANES), f32)],
        flops=12 * block * block * width,
    )(t, at, rows, cols, tot, got)


def exact_parts(value, rows):
    line = lax.broadcasted_iota(jnp.int32, (rows, value.shape[1]), 0)
    rest = jnp.broadcast_to(value, line.shape)
    out = jnp.zeros(line.shape, f32)
    for i in range(3):
        part = rest.astype(bf16).astype(f32)
        out = jnp.where(line == i, part, out)
        rest = rest - part
    return out


def embed_kernel(
    n_row, n_col, scale, t_ref, at_ref, rows_ref, cols_hbm, emb_hbm, unit_hbm, w_ref, tot_ref, got_ref, out_ref, cols_ref, emb_ref, unit_ref, sems
):
    pairs = ((cols_hbm, cols_ref), (emb_hbm, emb_ref), (unit_hbm, unit_ref))
    loads = [pltpu.make_async_copy(*pair, sems.at[i]) for i, pair in enumerate(pairs)]
    for load in loads:
        load.start()
    copies, parts = out_ref.shape[0], out_ref.shape[1]
    own, width = emb_ref.shape[1], emb_ref.shape[2]
    quarter = width // parts
    sums = [jnp.zeros((own, width), f32) for _ in range(2)]
    for i in range(rows_ref.shape[0]):
        for m in range(2):
            sums[m] += rows_ref[i, m].astype(f32)
    for load in loads:
        load.wait()
    d_unit = [sums[0], sums[1] + cols_ref[0].astype(f32), cols_ref[1].astype(f32)]
    unit = [unit_ref[m].astype(f32) for m in range(3)]
    for p, (a, b) in enumerate(couples):
        t = t_ref[p]
        score = t * jnp.sum(unit[a] * unit[b], axis=1, keepdims=True)
        g = (jnp.exp(score - t) * w_ref[p][:, 0:1] - 1.0).astype(bf16).astype(f32)
        d_unit[a] += (t * g) * unit[b]
        d_unit[b] += (t * g) * unit[a]
    for m in range(3):
        values = emb_ref[m].astype(f32)
        length = jnp.sqrt(jnp.sum(values * values, axis=1, keepdims=True) + epsilon)
        value = values / length
        inner = jnp.sum(value * d_unit[m], axis=1, keepdims=True)
        d = ((d_unit[m] - value * inner) / length).astype(bf16)
        for c in range(copies):
            for e in range(parts):
                out_ref[c, e, m * own : (m + 1) * own, :] = d[:, e * quarter : (e + 1) * quarter]
    row, col = softmax_sums(at_ref, tot_ref, got_ref)
    loss = -2.0 / n_row * row[3:4, 0:1]
    for p in range(3):
        for sums_of, count in ((row, n_row), (col, n_col)):
            lse = t_ref[p] + jnp.log(sums_of[p : p + 1])
            loss += jnp.sum(lse, axis=1, keepdims=True) * (1.0 / count)
    tail = exact_parts(jnp.broadcast_to(loss * scale, (1, quarter)), 16).astype(bf16)
    for c in range(copies):
        for e in range(parts):
            out_ref[c, e, 3 * own : 3 * own + 16, :] = tail


def embed_gradients(t, at, rows, cols, emb, unit, w, tot, got, copies, parts, total):
    _, own, width = emb.shape
    shape = (copies, parts, 3 * own + 16, width // parts)
    kernel = functools.partial(
        embed_kernel, tot.shape[1] // own, tot.shape[1] // own, 1.0 / (2 * total)
    )
    arrays = (rows, far_memory(cols), far_memory(emb), far_memory(unit), w, tot, got)
    return call(
        kernel,
        (1,),
        [scalars, scalars, whole(rows.shape)] + [remote] * 3 + [whole(x.shape) for x in (w, tot, got)],
        whole(shape),
        jax.ShapeDtypeStruct(shape, bf16),
        [pltpu.VMEM(x.shape, bf16) for x in (cols, emb, unit)] + [pltpu.SemaphoreType.DMA((3,))],
        flops=10**6,
    )(t, at, *arrays)


def head_kernel(share, line, at_ref, d_ref, own_ref, mine_ref, other_ref, out_ref):
    n_y = 1 + mine_ref.shape[0]
    my_core, my_y = at_ref[2], at_ref[3]
    n_far, height, quarter = out_ref.shape
    n_z = n_far // 2
    parts = d_ref.shape[0] // n_y
    own = (d_ref.shape[1] - 16) // 3
    clips = parts * own
    tail = jnp.sum(d_ref[:, 3 * own : 3 * own + 16, :].astype(f32), axis=0)
    loss = exact_parts(jnp.sum(tail, axis=0, keepdims=True), 8)[: height - 3 * share]
    totals = []
    for m in range(3):
        there = [
            d_ref[
                pl.ds(lax.rem(my_y + (n_y - step), n_y) * parts, parts), m * own : (m + 1) * own, :
            ].reshape(clips, quarter)
            for step in range(n_y)
        ]
        there = jnp.concatenate(there, axis=0)
        mine = [mine_ref[step, m] for step in range(n_y - 1)]
        other = [other_ref[step, m] for step in range(n_y - 1)]
        for x in range(2):
            here = [jnp.where(my_core == x, a, b) for a, b in zip(mine, other)]
            here = jnp.concatenate([own_ref[x, m]] + here, axis=1)
            totals.append(contract(here, there, ((1,), (0,))))
    for far in range(n_far):
        x, z = far // n_z, far % n_z
        piece = [totals[2 * m + x][z * line : z * line + share] for m in range(3)]
        out_ref[far] = jnp.concatenate(piece + [loss], axis=0).astype(bf16)


def head_gradients(at, d, own, mine, other, share, line):
    n_z = own.shape[2] // line
    quarter = d.shape[2]
    shape = (2 * n_z, -(-(3 * share + 3) // 16) * 16, quarter)
    return call(
        functools.partial(head_kernel, share, line),
        (1,),
        [scalars] + [whole(x.shape) for x in (d, own, mine, other)],
        whole(shape),
        jax.ShapeDtypeStruct(shape, bf16),
        flops=10**9,
    )(at, d, own, mine, far_memory(other))


def total_kernel(share, in_ref, loss_ref, *out_refs):
    total = jnp.zeros(in_ref.shape[1:], f32)
    for i in range(in_ref.shape[0]):
        total += in_ref[i].astype(f32)
    for m, ref in enumerate(out_refs):
        ref[...] = total[m * share : (m + 1) * share]
    loss = jnp.sum(total[3 * share : 3 * share + 3], axis=0, keepdims=True)
    loss_ref[...] = loss[:, 0:1]


def totals(pieces, share):
    shapes = [(1, 1)] + [(share, pieces.shape[2])] * 3
    return call(
        functools.partial(total_kernel, share),
        (1,),
        [whole(pieces.shape)],
        [whole(x) for x in shapes],
        [jax.ShapeDtypeStruct(x, f32) for x in shapes],
        flops=10**6,
    )(pieces)


def summing_groups(n_y, n_x, n_z, n_l):
    ids = np.arange(n_y * n_x * n_z * n_l * 2).reshape(n_y, n_x, n_z, n_l, 2)
    over_z = ids[..., 0].reshape(n_y * n_x, n_z * n_l)
    over_plane = ids[..., 1].transpose(2, 0, 1, 3).reshape(n_z, n_y * n_x * n_l)
    return over_z.tolist() + over_plane.tolist()


def shards(f0, f1, f2, h0, h1, h2, sharpness):
    features, heads = (f0, f1, f2), (h0, h1, h2)
    clips, feat = f0.shape
    quarter = h0.shape[1]
    emb_size = lax.axis_size(EMB)
    n_y, n_x, n_z = lax.axis_size("y"), lax.axis_size("xh"), lax.axis_size("z")
    n_row = lax.axis_size(ROW)
    own = clips // emb_size
    block_r = n_row * own
    at = jnp.stack(
        [lax.axis_index(axes) for axes in (ROW, COL, "core", "y", "xh", "xl")]
    ).astype(jnp.int32)

    share = feat // n_y // n_x // n_z
    line = -(-share // 8) * 8
    swap = [(0, 1), (1, 0)]
    wide, *sent = feature_shares(at, features, n_y, n_z, line)
    sent = [
        lax.ppermute(piece, "y", [(i, (i + step) % n_y) for i in range(n_y)])
        for step, piece in enumerate(sent, 1)
    ]
    mine = jnp.stack(sent)

    emb = project(features, heads, emb_size)
    emb, unit, cols, rows, own_scores = units(sharpness, exchange(emb, EMB))

    cols = lax.all_gather(cols, COL, axis=0)
    rows = exchange(copies_of(rows, n_row), ROW)
    rows, wide, mine = lax.optimization_barrier((rows, wide, mine))
    other = lax.ppermute(mine, "core", swap)

    send, keep = scores(sharpness, at, rows, cols, own_scores)
    send, keep, other = lax.optimization_barrier((send, keep, other))
    both = small(gather_kernel, at, (keep, lax.ppermute(send, "core", swap)), (n_row, 8, block_r))
    groups = summing_groups(n_y, n_x, n_z, 2)
    both = lax.all_to_all(
        both, ("y", "xh", "z", "xl", "core"), 0, 0, axis_index_groups=groups, tiled=True
    )
    tot = small(sum_kernel, at, (both,), (8, block_r))
    got = lax.ppermute(tot, "core", swap)

    grad, keep, send, w = products(sharpness, at, rows, cols, tot, got)
    received = lax.ppermute(send, "core", swap)
    d_rows = row_products(sharpness, grad, cols)
    received, d_rows = lax.optimization_barrier((received, d_rows))
    d_cols = (keep.astype(f32) + received.astype(f32)).astype(bf16)
    d_cols = lax.psum_scatter(d_cols, "z", scatter_dimension=0)
    d_rows = exchange(d_rows, ROW)

    d_emb = embed_gradients(
        sharpness, at, d_rows, d_cols, emb, unit, w, tot, got, n_y, emb_size, clips * lax.axis_size(DP)
    )
    d_emb = exchange(d_emb.reshape(n_y * emb_size, 3 * own + 16, quarter), NEAR)

    out = head_gradients(at, d_emb, wide, mine, other, share, line)
    loss, *out = totals(exchange(out, FAR), share)
    return loss.reshape(()), *out


def solution(mesh):
    fine = Mesh(mesh.devices.reshape(4, 2, 8, 2, 2), ("y", "xh", "z", "xl", "core"))
    clip_rows, columns = P(DP, None), P(None, EMB)
    out = P(DP, EMB)
    return jax.shard_map(
        shards,
        mesh=fine,
        in_specs=(clip_rows,) * 3 + (columns,) * 3 + (P(),),
        out_specs=(P(), out, out, out),
        check_vma=False,
    )
```

```python
import functools

import jax
import jax.numpy as jnp
import numpy as np
from jax import lax
from jax.experimental import pallas as pl
from jax.experimental.pallas import tpu as pltpu
from jax.sharding import Mesh, PartitionSpec as P

epsilon = 1e-06
couples = ((0, 1), (0, 2), (1, 2))
EMB = ("xl", "core")
DP = ("y", "xh", "z")
ROW = ("y", "xh", "xl")
COL = ("z", "core")
NEAR = ("y", "xl", "core")
FAR = ("xh", "z")
bf16 = jnp.bfloat16
f32 = jnp.float32
LANES = 128


def exchange(pieces, axes):
    return lax.all_to_all(pieces, axes, split_axis=0, concat_axis=0, tiled=True)


def contract(left, right, dims):
    return lax.dot_general(left, right, (dims, ((), ())), preferred_element_type=f32)


def call(kernel, grid, in_specs, out_specs, out_shape, scratch=(), flops=0, room=32):
    return pl.pallas_call(
        kernel,
        grid=grid,
        in_specs=in_specs,
        out_specs=out_specs,
        out_shape=out_shape,
        scratch_shapes=scratch,
        compiler_params=pltpu.CompilerParams(vmem_limit_bytes=room * 2**20),
        cost_estimate=pl.CostEstimate(flops=flops, bytes_accessed=8 * 2**20, transcendentals=0),
    )


def whole(shape):
    return pl.BlockSpec(shape, lambda *_: (0,) * len(shape))


scalars = pl.BlockSpec(memory_space=pltpu.SMEM)
remote = pl.BlockSpec(memory_space=pltpu.HBM)


def share_kernel(share, line, at_ref, f0_ref, f1_ref, f2_ref, own_ref, *send_refs):
    n_y = 1 + len(send_refs)
    rows, feat = own_ref.shape[2], f0_ref.shape[1]
    r = lax.broadcasted_iota(jnp.int32, (rows, 1), 0)
    place = r // line
    inside = r - place * line < share
    column = lax.broadcasted_iota(jnp.int32, (rows, feat), 1)
    jobs = [(own_ref.at[x], 0, x) for x in range(2)]
    jobs += [(ref, step, at_ref[2]) for step, ref in enumerate(send_refs, 1)]
    for ref, step, x in jobs:
        start = (2 * lax.rem(at_ref[3] + step, n_y) + x) * (feat // n_y // 2)
        target = jnp.where(inside, r - place * (line - share) + start, -1)
        pick = jnp.where(column == target, 1.0, 0.0).astype(bf16)
        for m, f_ref in enumerate((f0_ref, f1_ref, f2_ref)):
            ref[m] = contract(pick, f_ref[...], ((1,), (1,))).astype(bf16)


def feature_shares(at, features, n_y, n_z, line):
    clips, feat = features[0].shape
    share = feat // n_y // n_z // 2
    shape = (3, n_z * line, clips)
    shapes = [(2, *shape)] + [shape] * (n_y - 1)
    return call(
        functools.partial(share_kernel, share, line),
        (1,),
        [scalars] + [whole(f.shape) for f in features],
        [whole(x) for x in shapes],
        [pltpu.HBM(x, bf16) for x in shapes],
        flops=6 * n_y * n_z * line * feat * clips,
    )(at, *features)


def project_kernel(*refs):
    arrays, out_ref, buffers, sems = refs[:6], refs[6], refs[7:13], refs[13]
    parts, _, own, quarter = out_ref.shape
    copies = [pltpu.make_async_copy(arrays[i], buffers[i], sems.at[i]) for i in range(6)]
    for m in range(3):
        copies[m].start()
        copies[3 + m].start()
    for m in range(3):
        copies[m].wait()
        copies[3 + m].wait()
        emb = contract(buffers[m][...], buffers[3 + m][...], ((1,), (0,))).astype(bf16)
        out_ref[:, m] = emb.reshape(parts, own, quarter)


def project(features, heads, parts):
    clips, quarter = features[0].shape[0], heads[0].shape[1]
    shape = (parts, 3, clips // parts, quarter)
    arrays = features + heads
    return call(
        project_kernel,
        (1,),
        [remote] * 6,
        whole(shape),
        jax.ShapeDtypeStruct(shape, bf16),
        [pltpu.VMEM(x.shape, bf16) for x in arrays] + [pltpu.SemaphoreType.DMA((6,))],
        flops=10**8,
    )(*[far_memory(x) for x in arrays])


def unit_kernel(t_ref, emb_ref, all_ref, unit_ref, cols_ref, rows_ref, own_ref):
    parts, _, own, quarter = emb_ref.shape
    units = []
    for m in range(3):
        emb = jnp.concatenate([emb_ref[e, m] for e in range(parts)], axis=1)
        values = emb.astype(f32)
        length = jnp.sqrt(jnp.sum(values * values, axis=1, keepdims=True) + epsilon)
        unit = (values / length).astype(bf16)
        all_ref[m] = emb
        unit_ref[m] = unit
        units.append(unit.astype(f32))
        if m > 0:
            cols_ref[m - 1] = unit
        if m < 2:
            rows_ref[m] = unit
    total = jnp.zeros((1, parts * quarter), f32)
    for p, (a, b) in enumerate(couples):
        total += t_ref[p] * jnp.sum(units[a] * units[b], axis=0, keepdims=True)
    own_ref[...] = jnp.broadcast_to(jnp.sum(total, axis=1, keepdims=True), own_ref.shape)


def units(t, emb):
    parts, _, own, quarter = emb.shape
    full = (3, own, parts * quarter)
    two = (2, *full[1:])
    return call(
        unit_kernel,
        (1,),
        [scalars, whole(emb.shape)],
        [whole(x) for x in (full, full, two, two, (8, LANES))],
        [pltpu.HBM(x, bf16) for x in (full, full, two)]
        + [jax.ShapeDtypeStruct(two, bf16), jax.ShapeDtypeStruct((8, LANES), f32)],
        flops=10**6,
    )(t, emb)


def copies_kernel(in_ref, out_ref):
    for i in range(out_ref.shape[0]):
        out_ref[i] = in_ref[...]


def copies_of(value, count):
    zeros = (0,) * value.ndim
    return call(
        copies_kernel,
        (2,),
        [whole(value.shape)],
        pl.BlockSpec((count // 2, *value.shape), lambda i: (i, *zeros)),
        pltpu.HBM((count, *value.shape), value.dtype),
        flops=10**6,
    )(value)


def far_memory(value):
    return pltpu.with_memory_space_constraint(value, pltpu.HBM)


def shifted_scores(t, rows, cols):
    return jnp.exp(t * contract(rows, cols, ((1,), (1,))) - t)


def score_kernel(t_ref, at_ref, rows_ref, cols_hbm, own_ref, send_ref, keep_ref, cols_ref, sems):
    n_row, _, own, width = rows_ref.shape
    block = n_row * own
    copies = [pltpu.make_async_copy(cols_hbm.at[:, m], cols_ref.at[m], sems.at[m]) for m in range(2)]
    for copy in copies:
        copy.start()
    rows = [rows_ref[:, m].reshape(block, width) for m in range(2)]
    row_sums, col_sums = [], []
    for p, (a, b) in enumerate(((0, 0), (0, 1), (1, 1))):
        if p < 2:
            copies[p].wait()
        e = shifted_scores(t_ref[p], rows[a], cols_ref[b].reshape(block, width))
        col_sums.append(jnp.sum(e, axis=0, keepdims=True))
        total = jnp.broadcast_to(jnp.sum(e, axis=1, keepdims=True), (block, LANES))
        row_sums.append(total.T[0:1])
    own_sum = jnp.broadcast_to(own_ref[:, 0:1], (8, block))
    row = jnp.concatenate(row_sums + [own_sum[0:5]], axis=0)
    col = jnp.concatenate(col_sums + [own_sum[0:5]], axis=0)
    first = at_ref[2] == 0
    send_ref[...] = jnp.where(first, row, col)
    keep_ref[...] = jnp.where(first, col, row)


def scores(t, at, rows, cols, own_scores):
    n_row, _, own, width = rows.shape
    block = n_row * own
    return call(
        score_kernel,
        (1,),
        [scalars, scalars, whole(rows.shape), remote, whole(own_scores.shape)],
        [whole((8, block))] * 2,
        [jax.ShapeDtypeStruct((8, block), f32)] * 2,
        [pltpu.VMEM((2, n_row, own, width), bf16), pltpu.SemaphoreType.DMA((2,))],
        flops=6 * block * block * width,
    )(t, at, rows, far_memory(cols), own_scores)


def gather_kernel(at_ref, keep_ref, got_ref, out_ref):
    first = at_ref[2] == 0
    keep, got = keep_ref[...], got_ref[...]
    top = jnp.where(first, keep + got, got)[0:4]
    both = jnp.concatenate([top, keep[0:4]], axis=0)
    for copy in range(out_ref.shape[0]):
        out_ref[copy] = both


def sum_kernel(at_ref, both_ref, out_ref):
    first = at_ref[2] == 0
    out = jnp.zeros(out_ref.shape, f32)
    for i in range(both_ref.shape[0]):
        out += jnp.where(jnp.logical_and(first, at_ref[5] != i % 2), 0.0, both_ref[i])
    out_ref[...] = out


def small(kernel, at, arrays, shape):
    return call(
        kernel,
        (1,),
        [scalars] + [whole(x.shape) for x in arrays],
        whole(shape),
        jax.ShapeDtypeStruct(shape, f32),
        flops=10**5,
    )(at, *arrays)


def softmax_sums(at_ref, tot_ref, got_ref):
    first = at_ref[2] == 0
    row = jnp.where(first, got_ref[0:4], tot_ref[4:8])
    col = jnp.where(first, tot_ref[0:4], got_ref[0:4])
    return row, col


def product_kernel(
    t_ref, at_ref, rows_ref, cols_ref, tot_ref, got_ref, g_ref, keep_ref, send_ref, w_ref, hr_ref
):
    n_row, _, own, width = rows_ref.shape
    block = n_row * own
    my_row, my_col, my_core = at_ref[0], at_ref[1], at_ref[2]
    row, col = softmax_sums(at_ref, tot_ref, got_ref)
    row, col = 0.5 / row, 0.5 / col
    for p in range(3):
        hr_ref[p] = jnp.broadcast_to(row[p : p + 1], (LANES, block)).T
        hr_ref[3] = jnp.broadcast_to(col[p : p + 1], (LANES, block)).T
        w_ref[p] = (
            hr_ref[p, pl.ds(pl.multiple_of(my_row * own, own), own), :]
            + hr_ref[3, pl.ds(pl.multiple_of(my_col * own, own), own), :]
        )

    rows = [rows_ref[:, m].reshape(block, width) for m in range(2)]
    cols = [cols_ref[:, m].reshape(block, width) for m in range(2)]
    row_id = lax.broadcasted_iota(jnp.int32, (block, block), 0) - my_row * own
    col_id = lax.broadcasted_iota(jnp.int32, (block, block), 1) - my_col * own
    own_term = (row_id == col_id) & (row_id >= 0) & (row_id < own)
    grads = []
    for p, (a, b) in enumerate(((0, 0), (0, 1), (1, 1))):
        half = jnp.concatenate([hr_ref[p]] * (block // LANES), axis=1)
        g = shifted_scores(t_ref[p], rows[a], cols[b]) * (half + col[p : p + 1])
        grads.append(jnp.where(own_term, 0.0, g).astype(bf16))
        g_ref[p] = grads[p]
    d1 = t_ref[0] * contract(grads[0], rows[0], ((0,), (0,)))
    d2 = t_ref[1] * contract(grads[1], rows[0], ((0,), (0,)))
    d2 += t_ref[2] * contract(grads[2], rows[1], ((0,), (0,)))
    for m, d in enumerate((d1, d2)):
        for i in range(block // (2 * own)):
            low = d[2 * i * own : (2 * i + 1) * own]
            high = d[(2 * i + 1) * own : (2 * i + 2) * own]
            keep_ref[i, m] = jnp.where(my_core == 0, low, high).astype(bf16)
            send_ref[i, m] = jnp.where(my_core == 0, high, low).astype(bf16)


def row_kernel(t_ref, g_ref, cols_ref, out_hbm, out_ref, sems):
    n_row, own, width = out_ref.shape[1:]
    cols = [cols_ref[:, m].reshape(cols_ref.shape[0] * own, width) for m in range(2)]
    d0 = t_ref[0] * contract(g_ref[0], cols[0], ((1,), (0,)))
    d0 += t_ref[1] * contract(g_ref[1], cols[1], ((1,), (0,)))
    copies = []
    for m in range(2):
        d = d0 if m == 0 else t_ref[2] * contract(g_ref[2], cols[1], ((1,), (0,)))
        out_ref[m] = d.astype(bf16).reshape(n_row, own, width)
        copies.append(pltpu.make_async_copy(out_ref.at[m], out_hbm.at[:, m], sems.at[m]))
        copies[m].start()
    for copy in copies:
        copy.wait()


def row_products(t, g, cols):
    n_row, _, own, width = cols.shape
    return call(
        row_kernel,
        (1,),
        [scalars, whole(g.shape), whole(cols.shape)],
        remote,
        pltpu.HBM(cols.shape, bf16),
        [pltpu.VMEM((2, n_row, own, width), bf16), pltpu.SemaphoreType.DMA((2,))],
        flops=6 * (n_row * own) ** 2 * width,
    )(t, g, cols)


def products(t, at, rows, cols, tot, got):
    n_row, _, own, width = rows.shape
    block = n_row * own
    half = (n_row // 2, 2, own, width)
    return call(
        product_kernel,
        (1,),
        [scalars, scalars] + [whole(x.shape) for x in (rows, cols, tot, got)],
        [whole((3, block, block)), whole(half), whole(half), whole((3, own, LANES))],
        [
            jax.ShapeDtypeStruct((3, block, block), bf16),
            jax.ShapeDtypeStruct(half, bf16),
            jax.ShapeDtypeStruct(half, bf16),
            jax.ShapeDtypeStruct((3, own, LANES), f32),
        ],
        [pltpu.VMEM((4, block, LANES), f32)],
        flops=12 * block * block * width,
    )(t, at, rows, cols, tot, got)


def exact_parts(value, rows):
    line = lax.broadcasted_iota(jnp.int32, (rows, value.shape[1]), 0)
    rest = jnp.broadcast_to(value, line.shape)
    out = jnp.zeros(line.shape, f32)
    for i in range(3):
        part = rest.astype(bf16).astype(f32)
        out = jnp.where(line == i, part, out)
        rest = rest - part
    return out


def embed_kernel(
    n_row, n_col, scale, t_ref, at_ref, rows_ref, cols_hbm, emb_hbm, unit_hbm, w_ref, tot_ref, got_ref, out_ref, cols_ref, emb_ref, unit_ref, sems
):
    pairs = ((cols_hbm, cols_ref), (emb_hbm, emb_ref), (unit_hbm, unit_ref))
    loads = [pltpu.make_async_copy(*pair, sems.at[i]) for i, pair in enumerate(pairs)]
    for load in loads:
        load.start()
    copies, parts = out_ref.shape[0], out_ref.shape[1]
    own, width = emb_ref.shape[1], emb_ref.shape[2]
    quarter = width // parts
    sums = [jnp.zeros((own, width), f32) for _ in range(2)]
    for i in range(rows_ref.shape[0]):
        for m in range(2):
            sums[m] += rows_ref[i, m].astype(f32)
    for load in loads:
        load.wait()
    d_unit = [sums[0], sums[1] + cols_ref[0].astype(f32), cols_ref[1].astype(f32)]
    unit = [unit_ref[m].astype(f32) for m in range(3)]
    for p, (a, b) in enumerate(couples):
        t = t_ref[p]
        score = t * jnp.sum(unit[a] * unit[b], axis=1, keepdims=True)
        g = (jnp.exp(score - t) * w_ref[p][:, 0:1] - 1.0).astype(bf16).astype(f32)
        d_unit[a] += (t * g) * unit[b]
        d_unit[b] += (t * g) * unit[a]
    for m in range(3):
        values = emb_ref[m].astype(f32)
        length = jnp.sqrt(jnp.sum(values * values, axis=1, keepdims=True) + epsilon)
        value = values / length
        inner = jnp.sum(value * d_unit[m], axis=1, keepdims=True)
        d = ((d_unit[m] - value * inner) / length).astype(bf16)
        for c in range(copies):
            for e in range(parts):
                out_ref[c, e, m * own : (m + 1) * own, :] = d[:, e * quarter : (e + 1) * quarter]
    row, col = softmax_sums(at_ref, tot_ref, got_ref)
    loss = -2.0 / n_row * row[3:4, 0:1]
    for p in range(3):
        for sums_of, count in ((row, n_row), (col, n_col)):
            lse = t_ref[p] + jnp.log(sums_of[p : p + 1])
            loss += jnp.sum(lse, axis=1, keepdims=True) * (1.0 / count)
    tail = exact_parts(jnp.broadcast_to(loss * scale, (1, quarter)), 16).astype(bf16)
    for c in range(copies):
        for e in range(parts):
            out_ref[c, e, 3 * own : 3 * own + 16, :] = tail


def embed_gradients(t, at, rows, cols, emb, unit, w, tot, got, copies, parts, total):
    _, own, width = emb.shape
    shape = (copies, parts, 3 * own + 16, width // parts)
    kernel = functools.partial(
        embed_kernel, tot.shape[1] // own, tot.shape[1] // own, 1.0 / (2 * total)
    )
    arrays = (rows, far_memory(cols), far_memory(emb), far_memory(unit), w, tot, got)
    return call(
        kernel,
        (1,),
        [scalars, scalars, whole(rows.shape)] + [remote] * 3 + [whole(x.shape) for x in (w, tot, got)],
        whole(shape),
        jax.ShapeDtypeStruct(shape, bf16),
        [pltpu.VMEM(x.shape, bf16) for x in (cols, emb, unit)] + [pltpu.SemaphoreType.DMA((3,))],
        flops=10**6,
    )(t, at, *arrays)


def head_kernel(share, line, at_ref, d_ref, own_ref, mine_ref, other_ref, out_ref):
    n_y = 1 + mine_ref.shape[0]
    my_core, my_y = at_ref[2], at_ref[3]
    n_far, height, quarter = out_ref.shape
    n_z = n_far // 2
    parts = d_ref.shape[0] // n_y
    own = (d_ref.shape[1] - 16) // 3
    clips = parts * own
    tail = jnp.sum(d_ref[:, 3 * own : 3 * own + 16, :].astype(f32), axis=0)
    loss = exact_parts(jnp.sum(tail, axis=0, keepdims=True), 8)[: height - 3 * share]
    totals = []
    for m in range(3):
        there = [
            d_ref[
                pl.ds(lax.rem(my_y + (n_y - step), n_y) * parts, parts), m * own : (m + 1) * own, :
            ].reshape(clips, quarter)
            for step in range(n_y)
        ]
        there = jnp.concatenate(there, axis=0)
        mine = [mine_ref[step, m] for step in range(n_y - 1)]
        other = [other_ref[step, m] for step in range(n_y - 1)]
        for x in range(2):
            here = [jnp.where(my_core == x, a, b) for a, b in zip(mine, other)]
            here = jnp.concatenate([own_ref[x, m]] + here, axis=1)
            totals.append(contract(here, there, ((1,), (0,))))
    for far in range(n_far):
        x, z = far // n_z, far % n_z
        piece = [totals[2 * m + x][z * line : z * line + share] for m in range(3)]
        out_ref[far] = jnp.concatenate(piece + [loss], axis=0).astype(bf16)


def head_gradients(at, d, own, mine, other, share, line):
    n_z = own.shape[2] // line
    quarter = d.shape[2]
    shape = (2 * n_z, -(-(3 * share + 3) // 16) * 16, quarter)
    return call(
        functools.partial(head_kernel, share, line),
        (1,),
        [scalars] + [whole(x.shape) for x in (d, own, mine, other)],
        whole(shape),
        jax.ShapeDtypeStruct(shape, bf16),
        flops=10**9,
    )(at, d, own, mine, other)


def total_kernel(share, in_ref, loss_ref, *out_refs):
    total = jnp.zeros(in_ref.shape[1:], f32)
    for i in range(in_ref.shape[0]):
        total += in_ref[i].astype(f32)
    for m, ref in enumerate(out_refs):
        ref[...] = total[m * share : (m + 1) * share]
    loss = jnp.sum(total[3 * share : 3 * share + 3], axis=0, keepdims=True)
    loss_ref[...] = loss[:, 0:1]


def totals(pieces, share):
    shapes = [(1, 1)] + [(share, pieces.shape[2])] * 3
    return call(
        functools.partial(total_kernel, share),
        (1,),
        [whole(pieces.shape)],
        [whole(x) for x in shapes],
        [jax.ShapeDtypeStruct(x, f32) for x in shapes],
        flops=10**6,
    )(pieces)


def summing_groups(n_y, n_x, n_z, n_l):
    ids = np.arange(n_y * n_x * n_z * n_l * 2).reshape(n_y, n_x, n_z, n_l, 2)
    over_z = ids[..., 0].reshape(n_y * n_x, n_z * n_l)
    over_plane = ids[..., 1].transpose(2, 0, 1, 3).reshape(n_z, n_y * n_x * n_l)
    return over_z.tolist() + over_plane.tolist()


def shards(f0, f1, f2, h0, h1, h2, sharpness):
    features, heads = (f0, f1, f2), (h0, h1, h2)
    clips, feat = f0.shape
    quarter = h0.shape[1]
    emb_size = lax.axis_size(EMB)
    n_y, n_x, n_z = lax.axis_size("y"), lax.axis_size("xh"), lax.axis_size("z")
    n_row = lax.axis_size(ROW)
    own = clips // emb_size
    block_r = n_row * own
    at = jnp.stack(
        [lax.axis_index(axes) for axes in (ROW, COL, "core", "y", "xh", "xl")]
    ).astype(jnp.int32)

    share = feat // n_y // n_x // n_z
    line = -(-share // 8) * 8
    swap = [(0, 1), (1, 0)]
    wide, *sent = feature_shares(at, features, n_y, n_z, line)
    sent = [
        lax.ppermute(piece, "y", [(i, (i + step) % n_y) for i in range(n_y)])
        for step, piece in enumerate(sent, 1)
    ]
    mine = jnp.stack(sent)

    emb = project(features, heads, emb_size)
    emb, unit, cols, rows, own_scores = units(sharpness, exchange(emb, EMB))

    cols = lax.all_gather(cols, COL, axis=0)
    rows = exchange(copies_of(rows, n_row), ROW)
    rows, wide, mine = lax.optimization_barrier((rows, wide, mine))
    other = lax.ppermute(mine, "core", swap)

    send, keep = scores(sharpness, at, rows, cols, own_scores)
    send, keep, other = lax.optimization_barrier((send, keep, other))
    both = small(gather_kernel, at, (keep, lax.ppermute(send, "core", swap)), (n_row, 8, block_r))
    groups = summing_groups(n_y, n_x, n_z, 2)
    both = lax.all_to_all(
        both, ("y", "xh", "z", "xl", "core"), 0, 0, axis_index_groups=groups, tiled=True
    )
    tot = small(sum_kernel, at, (both,), (8, block_r))
    got = lax.ppermute(tot, "core", swap)

    grad, keep, send, w = products(sharpness, at, rows, cols, tot, got)
    received = lax.ppermute(send, "core", swap)
    d_rows = row_products(sharpness, grad, cols)
    received, d_rows = lax.optimization_barrier((received, d_rows))
    d_cols = (keep.astype(f32) + received.astype(f32)).astype(bf16)
    d_cols = lax.psum_scatter(d_cols, "z", scatter_dimension=0)
    d_rows = exchange(d_rows, ROW)

    d_emb = embed_gradients(
        sharpness, at, d_rows, d_cols, emb, unit, w, tot, got, n_y, emb_size, clips * lax.axis_size(DP)
    )
    d_emb = exchange(d_emb.reshape(n_y * emb_size, 3 * own + 16, quarter), NEAR)

    out = head_gradients(at, d_emb, wide, mine, other, share, line)
    loss, *out = totals(exchange(out, FAR), share)
    return loss.reshape(()), *out


def solution(mesh):
    fine = Mesh(mesh.devices.reshape(4, 2, 8, 2, 2), ("y", "xh", "z", "xl", "core"))
    clip_rows, columns = P(DP, None), P(None, EMB)
    out = P(DP, EMB)
    return jax.shard_map(
        shards,
        mesh=fine,
        in_specs=(clip_rows,) * 3 + (columns,) * 3 + (P(),),
        out_specs=(P(), out, out, out),
        check_vma=False,
    )
```
